128 devices in a mesh: dp: 4 (over y_hi, core), grp: 32 (over z, y_lo, x).
Axes of the slice: x: 4, y: 4 (y_hi: 2, y_lo: 2; y = y_hi * 2 + y_lo), z: 4, core: 2. Of those that a mesh axis runs over, the one named last changes fastest.
Arguments:
- token_ids: int32 [4, 4, 8, 4], P('dp'), may hold values from 0 to 128255
- start_pos: int32 [4, 4, 8], P('dp'), may hold values from 0 to 8191
- cache_len: int32 [4, 4, 8], P('dp'), may hold values from 1 to 1020, as said below
- embed_table: bfloat16 [128256, 4096], P(('dp', 'grp')), may hold values from -6 to 6
- norm_gain: float32 [2, 4096], replicated, may hold values from 0.1 to 1.9
- query_key_value_weight: bfloat16 [2, 4096, 6144], P(None, 'grp'), may hold values from -0.09375 to 0.09375
- output_weight: bfloat16 [2, 4096, 4096], P(None, 'grp'), may hold values from -0.09375 to 0.09375
- key_value_cache: bfloat16 [2, 32, 32, 1024, 256], P(None, 'dp', 'grp'), may hold values from -24 to 24, as said below
Outputs:
- decoded: bfloat16 [32, 32, 4, 512], P('dp', 'grp')
The draws below stay inside these ranges and needn't reach their ends.
Inputs may be any that keep to these rules, and one draw needn't show every extreme that they name: `cache_len`: in every draw some sequence has exactly 1020 live positions and some sequence has exactly 1. `key_value_cache`: keys are stored already rotated.
All inputs are finite; a program needn't handle non-finite values.
Results may differ from the reference program's by a relative error of at most 0.029.
Values may be sent and summed in bfloat16 or wider, within the bound.
A program may use at most 192 MiB of HBM per device.

```python
import math
import jax
import jax.numpy as jnp
import numpy as np
from jax import lax

MODEL_WIDTH = 4096
QUERY_HEADS = 32
KEY_VALUE_HEADS = 8
HEAD_SIZE = 128
VOCAB = 128256
DECODER_LAYERS = 2
DECODE_STEPS = 4
REPLICA_ROWS = 8
CACHE_POSITIONS = 1024
ROLLOUT_COPIES = 4
N_DP = 4


def draw_cache_len(key, part):
    key = jax.random.fold_in(key, 11)
    key_one, key_two, key_three = jax.random.split(key, 3)
    number = N_DP * ROLLOUT_COPIES * REPLICA_ROWS
    flat = jax.random.randint(key_one, (number,), 1, CACHE_POSITIONS - DECODE_STEPS + 1)
    top_place = jax.random.randint(key_two, (), 0, number)
    low_place = (top_place + 1 + jax.random.randint(key_three, (), 0, number - 1)) % number
    places = jnp.arange(number)
    flat = jnp.where(places == top_place, CACHE_POSITIONS - DECODE_STEPS, flat)
    flat = jnp.where(places == low_place, 1, flat)
    return flat.reshape(N_DP, ROLLOUT_COPIES, REPLICA_ROWS).astype(jnp.int32)


def draw_key_value_cache(key, part):
    key = jax.random.fold_in(key, 23)
    key_one = jax.random.fold_in(key, 0)
    target_shape = (DECODER_LAYERS, N_DP * REPLICA_ROWS, ROLLOUT_COPIES * KEY_VALUE_HEADS, CACHE_POSITIONS, 2 * HEAD_SIZE)
    values = jnp.clip(3.0 * jax.random.normal(key_one, target_shape, jnp.float32), -18.0, 18.0)
    return values.astype(jnp.bfloat16)


def with_ends(array, key, low, high):
    spot = [jax.random.randint(jax.random.fold_in(key, axis), (), 0, length) for axis, length in enumerate(array.shape)]
    main_axis = array.shape.index(max(array.shape))
    neighbour = spot[:main_axis] + [(spot[main_axis] + 1) % array.shape[main_axis]] + spot[main_axis + 1:]
    return array.at[tuple(spot)].set(low).at[tuple(neighbour)].set(high)


def shard_levels(stream_key, dims, cuts, low, largest):
    factor_of, own = 1.0, jax.random.fold_in(stream_key, 6)
    for dim, shards_of in cuts:
        steps = jnp.exp(jax.random.uniform(jax.random.fold_in(own, dim), (shards_of,), jnp.float32, low / len(cuts), largest / len(cuts)))
        factor_of = factor_of * jnp.repeat(steps, dims[dim] // shards_of).reshape([-1 if axis == dim else 1 for axis in range(len(dims))])
    return factor_of


def skewed_wide(rng, shape, amount, lean):
    portions = [min(1 << octave, amount + 1 - (1 << octave)) * (1 << 20) // math.isqrt((1 << octave) ** lean) + 1 for octave in range((amount + 1).bit_length()) if 1 << octave <= amount]
    width = 1 + sum(portions) // (1 << 30)
    grid = np.cumsum(np.array([max(1, weight // width) for weight in portions]))
    pick = jax.random.randint(jax.random.fold_in(rng, 1), shape, 0, int(grid[len(portions) - 1]))
    start = jnp.left_shift(1, jnp.searchsorted(jnp.asarray(grid, jnp.int32), pick, side="right").astype(jnp.int32))
    rank = start - 1 + jax.random.randint(jax.random.fold_in(rng, 4), shape, 0, 1 << 30) % jnp.minimum(start, amount + 1 - start)
    return jax.random.permutation(jax.random.fold_in(rng, 2), amount)[rank].astype(jnp.int32)


def bell_draw(key, extent, width, bound, cuts=(), held_as=jnp.bfloat16):
    drawn = jax.random.normal(key, extent, jnp.float32) * width
    if len(cuts) > 0:
        drawn = shard_levels(key, extent, cuts, -0.22, 0.18) * drawn
    return jnp.clip(drawn, min=-bound, max=bound).astype(held_as)


def setup_inputs(seed: int = 0) -> dict:
    streams_of = jax.random.split(jax.random.key(seed), 9)
    token_ids = with_ends(skewed_wide(streams_of[0], (N_DP, ROLLOUT_COPIES, REPLICA_ROWS, DECODE_STEPS), VOCAB, 2), jax.random.fold_in(streams_of[0], 3), 0, VOCAB - 1).astype(jnp.int32)
    start_pos = with_ends(jax.random.randint(streams_of[1], (N_DP, ROLLOUT_COPIES, REPLICA_ROWS), 0, 8192), jax.random.fold_in(streams_of[1], 1), 0, 8191).astype(jnp.int32)
    cache_len = draw_cache_len(jax.random.fold_in(streams_of[8], 71), 0)
    embed_table = bell_draw(streams_of[3], (VOCAB, MODEL_WIDTH), 1.0, 6.0, ((0, 128),))
    norm_gain = jnp.clip(1.0 + 0.18 * jax.random.normal(streams_of[4], (DECODER_LAYERS, MODEL_WIDTH), jnp.float32), 0.1, 1.9)
    query_key_value_weight = bell_draw(streams_of[5], (DECODER_LAYERS, MODEL_WIDTH, (QUERY_HEADS + 2 * KEY_VALUE_HEADS) * HEAD_SIZE), MODEL_WIDTH ** -0.5, 0.09375, ((1, 32),))
    output_weight = bell_draw(streams_of[6], (DECODER_LAYERS, MODEL_WIDTH, QUERY_HEADS * HEAD_SIZE), (QUERY_HEADS * HEAD_SIZE) ** -0.5, 0.09375, ((1, 32),))
    key_value_cache = draw_key_value_cache(jax.random.fold_in(streams_of[8], 71), 0)
    return {"token_ids": token_ids, "start_pos": start_pos, "cache_len": cache_len, "embed_table": embed_table, "norm_gain": norm_gain, "query_key_value_weight": query_key_value_weight, "output_weight": output_weight, "key_value_cache": key_value_cache}


ROPE_BASE = 500000.0
EPSILON = 1e-05

def rotate(vectors, position):
    half_width = vectors.shape[-1] // 2
    exponent = jnp.arange(half_width, dtype=jnp.float32) * (2.0 / vectors.shape[-1])
    frequency = jnp.power(jnp.float32(ROPE_BASE), -exponent)
    angles = position.astype(jnp.float32)[..., None] * frequency
    cosine = jnp.cos(angles)
    sine = jnp.sin(angles)
    first_half = vectors[..., :half_width]
    second_half = vectors[..., half_width:]
    return jnp.concatenate([first_half * cosine - second_half * sine, second_half * cosine + first_half * sine], axis=-1)

def rms_normed(stream, gain):
    factor = lax.rsqrt(lax.optimization_barrier(jnp.mean(stream * stream, axis=-1, keepdims=True)) + EPSILON)
    return (stream * factor * gain).astype(jnp.bfloat16)

def reference(token_ids, start_pos, cache_len, embed_table, norm_gain, query_key_value_weight, output_weight, key_value_cache):
    heads_per_group = QUERY_HEADS // KEY_VALUE_HEADS
    query_feature_width = QUERY_HEADS * HEAD_SIZE
    scale = HEAD_SIZE ** (-0.5)

    def one_group(group_index):
        replica_group_index = group_index // ROLLOUT_COPIES
        replica_number = group_index % ROLLOUT_COPIES
        row_ids = token_ids[replica_group_index, replica_number]
        starts = start_pos[replica_group_index, replica_number]
        lengths = cache_len[replica_group_index, replica_number]
        leading_zero_index = jnp.int32(0)
        layer_caches = lax.dynamic_slice(key_value_cache, (leading_zero_index, replica_group_index * REPLICA_ROWS, replica_number * KEY_VALUE_HEADS, leading_zero_index, leading_zero_index), (DECODER_LAYERS, REPLICA_ROWS, KEY_VALUE_HEADS, CACHE_POSITIONS, 2 * HEAD_SIZE))
        embedded = jnp.take(embed_table, row_ids, axis=0).astype(jnp.float32)
        incoming_keys = jnp.zeros((DECODER_LAYERS, REPLICA_ROWS, DECODE_STEPS, KEY_VALUE_HEADS, HEAD_SIZE), jnp.bfloat16)
        incoming_values = jnp.zeros((DECODER_LAYERS, REPLICA_ROWS, DECODE_STEPS, KEY_VALUE_HEADS, HEAD_SIZE), jnp.bfloat16)
        cache_ok = jnp.arange(CACHE_POSITIONS, dtype=jnp.int32)[None, :] < lengths[:, None]
        cache_mask = cache_ok[:, None, None, :]
        results = []
        for step_no in range(DECODE_STEPS):
            stream = embedded[:, step_no]
            positions = starts + step_no
            fresh_mask = (jnp.arange(DECODE_STEPS, dtype=jnp.int32) <= step_no)[None, None, None, :]
            for layer_no in range(DECODER_LAYERS):
                normed = rms_normed(stream, norm_gain[layer_no])
                projected_output = jnp.dot(normed, query_key_value_weight[layer_no], preferred_element_type=jnp.float32)
                query_rows = projected_output[:, :query_feature_width].reshape(REPLICA_ROWS, KEY_VALUE_HEADS, heads_per_group, HEAD_SIZE)
                current_keys = projected_output[:, query_feature_width:query_feature_width + KEY_VALUE_HEADS * HEAD_SIZE].reshape(REPLICA_ROWS, KEY_VALUE_HEADS, HEAD_SIZE)
                current_values = projected_output[:, query_feature_width + KEY_VALUE_HEADS * HEAD_SIZE:].reshape(REPLICA_ROWS, KEY_VALUE_HEADS, HEAD_SIZE)
                query_rows = rotate(query_rows, positions[:, None, None]).astype(jnp.bfloat16)
                current_keys = rotate(current_keys, positions[:, None]).astype(jnp.bfloat16)
                incoming_keys = incoming_keys.at[layer_no, :, step_no].set(current_keys)
                incoming_values = incoming_values.at[layer_no, :, step_no].set(current_values.astype(jnp.bfloat16))
                cache_keys = layer_caches[layer_no, :, :, :, :HEAD_SIZE].astype(jnp.float32)
                cache_values = layer_caches[layer_no, :, :, :, HEAD_SIZE:].astype(jnp.float32)
                query_wide = query_rows.astype(jnp.float32)
                cache_scores = jnp.einsum('rhgd,rhjd->rhgj', query_wide, cache_keys) * scale
                fresh_scores = jnp.einsum('rhgd,rjhd->rhgj', query_wide, incoming_keys[layer_no].astype(jnp.float32)) * scale
                cache_exp = jnp.where(cache_mask, jnp.exp(cache_scores), 0.0)
                fresh_exp = jnp.where(fresh_mask, jnp.exp(fresh_scores), 0.0)
                denominator = lax.optimization_barrier(jnp.sum(cache_exp, axis=-1, keepdims=True)) + lax.optimization_barrier(jnp.sum(fresh_exp, axis=-1, keepdims=True))
                cache_weights = (cache_exp / denominator).astype(jnp.bfloat16)
                fresh_weights = (fresh_exp / denominator).astype(jnp.bfloat16)
                attended = jnp.einsum('rhgj,rhjd->rhgd', cache_weights.astype(jnp.float32), cache_values)
                attended = attended + jnp.einsum('rhgj,rjhd->rhgd', fresh_weights.astype(jnp.float32), incoming_values[layer_no].astype(jnp.float32))
                attended = attended.astype(jnp.bfloat16).reshape(REPLICA_ROWS, query_feature_width)
                stream = stream + jnp.dot(attended, output_weight[layer_no].T, preferred_element_type=jnp.float32)
            results.append(stream.astype(jnp.bfloat16))
        return jnp.stack(results, axis=1)
    combined_heads = lax.map(one_group, jnp.arange(N_DP * ROLLOUT_COPIES, dtype=jnp.int32))
    reshaped_weight = combined_heads.reshape(N_DP, ROLLOUT_COPIES, REPLICA_ROWS, DECODE_STEPS, KEY_VALUE_HEADS, MODEL_WIDTH // KEY_VALUE_HEADS)
    return reshaped_weight.transpose(0, 2, 1, 4, 3, 5).reshape(N_DP * REPLICA_ROWS, ROLLOUT_COPIES * KEY_VALUE_HEADS, DECODE_STEPS, MODEL_WIDTH // KEY_VALUE_HEADS)
```

```python
import jax
import jax.numpy as jnp
from jax import lax
from jax.experimental import pallas as pl
from jax.experimental.pallas import tpu as pltpu
from jax.sharding import PartitionSpec as P

MODEL_WIDTH = 4096
QUERY_HEADS = 32
KEY_VALUE_HEADS = 8
HEAD_SIZE = 128
DECODER_LAYERS = 2
DECODE_STEPS = 4
REPLICA_ROWS = 8
ROPE_BASE = 500000.0
EPSILON = 1e-05

MESH = pl.DeviceIdType.MESH
SLOTS = 16
DP = 4
PLANES = 4
SLICES = 8
GRP = PLANES * SLICES
TOKENS = REPLICA_ROWS * DECODE_STEPS
ALL = PLANES * TOKENS
D = 128
QKV = 768
CACHE = 1024
FRESH_AT = CACHE - DECODE_STEPS
BF = jnp.bfloat16
F32 = jnp.float32


def ids_kernel(ids_ref, out_ref, land, send_sem, recv_sem):
    a, g = lax.axis_index("dp"), lax.axis_index("grp")
    barrier = pltpu.get_barrier_semaphore()
    for j in range(1, DP):
        pl.semaphore_signal(barrier, inc=1, device_id=((a + j) % DP, g), device_id_type=MESH)
    pl.semaphore_wait(barrier, DP - 1)
    copies = []
    for j in range(1, DP):
        copy = pltpu.make_async_remote_copy(
            src_ref=ids_ref,
            dst_ref=land.at[j],
            send_sem=send_sem.at[j],
            recv_sem=recv_sem.at[j],
            device_id=((a + j) % DP, g),
            device_id_type=MESH,
        )
        copy.start()
        copies.append(copy)
    out_ref[a] = ids_ref[...]
    for j in range(1, DP):
        copies[j - 1].wait()
        out_ref[(a - j + DP) % DP] = land[j]


def gather_ids(ids):
    return pl.pallas_call(
        ids_kernel,
        out_shape=jax.ShapeDtypeStruct((DP, 8, ALL), jnp.int32),
        in_specs=[pl.BlockSpec(memory_space=pltpu.VMEM)],
        out_specs=pl.BlockSpec(memory_space=pltpu.VMEM),
        scratch_shapes=[
            pltpu.VMEM((DP, 8, ALL), jnp.int32),
            pltpu.SemaphoreType.DMA((DP,)),
            pltpu.SemaphoreType.DMA((DP,)),
        ],
        compiler_params=pltpu.CompilerParams(collective_id=0, has_side_effects=True),
        name="gather_ids",
    )(jnp.broadcast_to(ids[None], (8, ALL)))


def main_kernel(
    rows_ref,
    idx_ref,
    extra_ref,
    gain_ref,
    cos_ref,
    sin_ref,
    len_ref,
    wq_ref,
    wo_ref,
    cache_ref,
    out_ref,
    cache_v,
    wqx,
    wox,
    ebuf,
    tbuf,
    dbuf,
    stream,
    p1s,
    p1r,
    p2s,
    p2r,
    qs,
    kvs,
    atts,
    p3s,
    p3r,
    p4s,
    p4r,
    pfs,
    pfr,
    cache_sem,
    w_send,
    w_recv,
    f_send,
    f_recv,
    e_send,
    e_recv,
    d_send,
    d_recv,
    p1_send,
    p1_recv,
    p2_send,
    p2_recv,
    p3_send,
    p3_recv,
    p4_send,
    p4_recv,
):
    a, g = lax.axis_index("dp"), lax.axis_index("grp")
    core = a % 2
    sibling = a + 1 - 2 * core
    z, t = g // SLICES, g % SLICES
    y, x = t // 4, t % 4

    def remote(src, dst, send_sem, recv_sem, a2, g2):
        return pltpu.make_async_remote_copy(
            src_ref=src,
            dst_ref=dst,
            send_sem=send_sem,
            recv_sem=recv_sem,
            device_id=(a2, g2),
            device_id_type=MESH,
        )

    def wait_bytes(ref, sem):
        pltpu.make_async_copy(ref, ref, sem).wait()

    def slice_at(j):
        return ((y + j // 4) % 2) * 4 + (x + j % 4) % 4

    for l in range(DECODER_LAYERS):
        pltpu.make_async_copy(cache_ref.at[l], cache_v.at[l], cache_sem.at[l]).start()

    barrier = pltpu.get_barrier_semaphore()

    def greet(j, c):
        pl.semaphore_signal(barrier, inc=1, device_id=(a, (g + j) % GRP), device_id_type=MESH)
        return c

    lax.fori_loop(1, GRP, greet, 0)
    for j in range(1, DP):
        pl.semaphore_signal(barrier, inc=1, device_id=((a + j) % DP, g), device_id_type=MESH)
    pl.semaphore_wait(barrier, GRP - 1 + DP - 1)

    def send_rows(j, c):
        g2 = ((z + j // SLICES) % PLANES) * SLICES + slice_at(j % SLICES)
        remote(rows_ref.at[g2], ebuf.at[g], e_send, e_recv, a, g2).start()
        return c

    lax.fori_loop(1, GRP, send_rows, 0)

    half = pl.ds(pl.multiple_of(core * 64, 64), 64)

    def qkv_pieces(l, t2):
        return (
            (
                wq_ref.at[l, half, pl.ds(pl.multiple_of(t2 * 512, 512), 512)],
                wqx.at[l, t, half, pl.ds(0, 512)],
            ),
            (
                wq_ref.at[l, half, pl.ds(pl.multiple_of(4096 + t2 * 128, 128), 128)],
                wqx.at[l, t, half, pl.ds(512, 128)],
            ),
            (
                wq_ref.at[l, half, pl.ds(pl.multiple_of(5120 + t2 * 128, 128), 128)],
                wqx.at[l, t, half, pl.ds(640, 128)],
            ),
        )

    def out_pieces(l, t2):
        return (
            (
                wo_ref.at[l, half, pl.ds(pl.multiple_of(t2 * 512, 512), 512)],
                wox.at[l, t, half, :],
            ),
        )

    def send_weights(l, kind):
        pieces = (qkv_pieces, out_pieces)[kind]

        def one(j, c):
            t2 = slice_at(j)
            for src, dst in pieces(l, t2):
                remote(src, dst, w_send.at[l, kind], w_recv.at[l, kind], a, z * SLICES + t2).start()
            return c

        lax.fori_loop(1, SLICES, one, 0)
        for src, dst in pieces(l, t):
            pltpu.make_async_copy(src, dst, w_recv.at[l, kind]).start()

    def forward_weights(l, kind):
        buf = (wqx, wox)[kind]
        wait_bytes(buf.at[l, :, half, :], w_recv.at[l, kind])
        remote(
            buf.at[l, :, half, :],
            buf.at[l, :, half, :],
            f_send.at[l, kind],
            f_recv.at[l, kind],
            sibling,
            g,
        ).start()

    def await_weights(l, kind):
        buf = (wqx, wox)[kind]
        wait_bytes(buf.at[l, :, half, :], f_recv.at[l, kind])

    send_weights(0, 0)
    ebuf[g] = rows_ref[g]
    kvs[...] = jnp.zeros_like(kvs)
    wait_bytes(ebuf.at[pl.ds(0, GRP - 1)], e_recv)
    table = ebuf[...].reshape(GRP * SLOTS, D)

    def picked(a2):
        want = idx_ref[pl.ds(pl.multiple_of(a2 * ALL, ALL), ALL), :]
        place = lax.broadcasted_iota(jnp.int32, (ALL, GRP * SLOTS), 1)
        chosen = jnp.where(place == want, 1.0, 0.0).astype(BF)
        return jnp.dot(chosen, table, preferred_element_type=F32)

    for j in range(1, DP):
        a2 = (a + j) % DP
        tbuf[j] = picked(a2).astype(BF)
        remote(tbuf.at[j], dbuf.at[j], d_send, d_recv, a2, g).start()
    send_weights(0, 1)
    mine = picked(a) + extra_ref[...]
    wait_bytes(dbuf.at[pl.ds(1, DP - 1)], d_recv)
    for j in range(1, DP):
        mine = mine + dbuf[j].astype(F32)
    stream[...] = mine

    row32 = lax.broadcasted_iota(jnp.int32, (TOKENS, ALL), 0)
    lane32 = lax.broadcasted_iota(jnp.int32, (TOKENS, ALL), 1)
    own_token = lane32 == row32 + z * TOKENS

    def split(value):
        high = value.astype(BF).astype(F32)
        return jnp.concatenate([high, value - high], axis=0).astype(BF)

    for l in range(DECODER_LAYERS):
        s = stream[...]
        square = s * s
        high = square.astype(BF)
        low = (square - high.astype(F32)).astype(BF)
        ones = jnp.ones((8, D), BF)
        contract = (((1,), (1,)), ((), ()))
        sums = lax.dot_general(ones, high, contract, preferred_element_type=F32)
        sums = sums + lax.dot_general(ones, low, contract, preferred_element_type=F32)
        p1s[l, 0:ALL, :] = (s * gain_ref[l]).astype(BF)
        p1s[l, ALL : ALL + 16, :] = split(sums)

        def send_stream(j, c):
            remote(
                p1s.at[l], p1r.at[l, t], p1_send.at[l], p1_recv.at[l], a, z * SLICES + slice_at(j)
            ).start()
            return c

        lax.fori_loop(1, SLICES, send_stream, 0)
        p1r[l, t] = p1s[l]
        forward_weights(l, 0)
        wait_bytes(p1r.at[l, pl.ds(0, SLICES - 1)], p1_recv.at[l])
        await_weights(l, 0)

        left = jnp.concatenate([p1r[l, j, 0:ALL, :] for j in range(SLICES)], axis=1)
        sums = jnp.zeros((8, ALL), F32)
        for j in range(SLICES):
            tile = p1r[l, j, ALL : ALL + 16, :].astype(F32)
            sums = sums + tile[0:8] + tile[8:16]
        projected = jnp.dot(
            left, wqx[l].reshape(SLICES * D, QKV), preferred_element_type=F32
        ).astype(BF)
        sums = split(sums)
        for r in range(PLANES):
            for c in range(QKV // D):
                p2s[l, r, c * TOKENS : (c + 1) * TOKENS, :] = projected[
                    r * TOKENS : (r + 1) * TOKENS, c * D : (c + 1) * D
                ]
            p2s[l, r, 192:208, :] = sums
        for j in range(1, PLANES):
            z2 = (z + j) % PLANES
            remote(
                p2s.at[l, z2], p2r.at[l, j], p2_send.at[l], p2_recv.at[l], a, z2 * SLICES + t
            ).start()
        forward_weights(l, 1)
        wait_bytes(p2r.at[l, pl.ds(1, PLANES - 1)], p2_recv.at[l])
        if l + 1 < DECODER_LAYERS:
            send_weights(l + 1, 0)
        total = p2s[l, z].astype(F32)
        for j in range(1, PLANES):
            total = total + p2r[l, j].astype(F32)

        line = total[192:193] + total[200:201]
        column = jnp.sum(
            jnp.where(own_token, jnp.broadcast_to(line, (TOKENS, ALL)), 0.0), axis=1, keepdims=True
        )
        factor = lax.rsqrt(column * (1.0 / MODEL_WIDTH) + EPSILON)
        cosine, sine = cos_ref[...], sin_ref[...]

        def rotated(block):
            return block * cosine + pltpu.roll(block, 64, 1) * sine

        for h in range(4):
            qs[h * TOKENS : (h + 1) * TOKENS, :] = rotated(
                total[h * TOKENS : (h + 1) * TOKENS] * factor
            )
        kvs[0, 96:128, :] = rotated(total[128:160] * factor)
        kvs[1, 96:128, :] = total[160:192] * factor
        pltpu.make_async_copy(cache_ref.at[l], cache_v.at[l], cache_sem.at[l]).wait()
        fresh_row = lax.broadcasted_iota(jnp.int32, (16, D), 0) >= 12
        place = lax.broadcasted_iota(jnp.int32, (16, CACHE), 1)
        step = lax.broadcasted_iota(jnp.int32, (16, CACHE), 0) % DECODE_STEPS
        fresh_live = (place >= FRESH_AT) & (place - FRESH_AT <= step)
        for b in range(REPLICA_ROWS):
            for k in range(2):
                old = cache_v[l, b, CACHE - 16 : CACHE, k * D : (k + 1) * D].astype(F32)
                new = kvs[k, pl.ds(b, 16, stride=8), :]
                cache_v[l, b, CACHE - 16 : CACHE, k * D : (k + 1) * D] = jnp.where(
                    fresh_row, new, old
                ).astype(BF)
        for b in range(REPLICA_ROWS):
            query = qs[pl.ds(b, 16, stride=8), :].astype(BF)
            scores = lax.dot_general(
                query, cache_v[l, b, :, 0:D], contract, preferred_element_type=F32
            ) * (HEAD_SIZE**-0.5)
            live = (place < len_ref[b]) | fresh_live
            scores = jnp.where(live, scores, -1e30)
            top = jnp.max(scores, axis=1, keepdims=True)
            power = jnp.exp(scores - top)
            whole = jnp.sum(power, axis=1, keepdims=True)
            value = jnp.dot(power.astype(BF), cache_v[l, b, :, D : 2 * D], preferred_element_type=F32)
            atts[pl.ds(b, 16, stride=8), :] = value / whole

        p3s[l] = atts[...].astype(BF)
        for j in range(1, PLANES):
            z2 = (z + j) % PLANES
            remote(
                p3s.at[l], p3r.at[l, z], p3_send.at[l], p3_recv.at[l], a, z2 * SLICES + t
            ).start()
        p3r[l, z] = p3s[l]
        await_weights(l, 1)
        wait_bytes(p3r.at[l, pl.ds(0, PLANES - 1)], p3_recv.at[l])
        if l + 1 < DECODER_LAYERS:
            send_weights(l + 1, 1)
        left = jnp.concatenate(
            [
                jnp.concatenate(
                    [p3r[l, r, h * TOKENS : (h + 1) * TOKENS, :] for r in range(PLANES)], axis=0
                )
                for h in range(4)
            ],
            axis=1,
        )

        def partial(t2):
            return lax.dot_general(left, wox[l, t2], contract, preferred_element_type=F32)

        if l + 1 < DECODER_LAYERS:

            for j in range(1, SLICES):
                t2 = slice_at(j)
                p4s[j] = partial(t2).astype(BF)
                remote(p4s.at[j], p4r.at[j], p4_send.at[0], p4_recv.at[0], a, z * SLICES + t2).start()
            s = stream[...] + partial(t)
            wait_bytes(p4r.at[pl.ds(1, SLICES - 1)], p4_recv.at[0])
            for j in range(1, SLICES):
                s = s + p4r[j].astype(F32)
            stream[...] = s
        else:
            for e in range(2):
                for k in range(4):
                    t2 = e * 4 + k
                    part = partial(t2)
                    part = part + jnp.where(t == t2, stream[...], 0.0)
                    part = part.astype(BF)
                    for r in range(PLANES):
                        pfs[r, e, :, k * D : (k + 1) * D] = part[r * TOKENS : (r + 1) * TOKENS]
                for j in range(PLANES):
                    r = (z + j) % PLANES
                    g2 = r * SLICES + 2 * z + e

                    @pl.when(g2 != g)
                    def _():
                        remote(
                            pfs.at[r, e], pfr.at[t], p4_send.at[1], p4_recv.at[1], a, g2
                        ).start()

                    @pl.when(g2 == g)
                    def _():
                        pltpu.make_async_copy(pfs.at[r, e], pfr.at[t], p4_recv.at[1]).start()

            wait_bytes(pfr, p4_recv.at[1])
            result = pfr[0].astype(F32)
            for j in range(1, SLICES):
                result = result + pfr[j].astype(F32)
            out_ref[...] = result.astype(BF)

    wait_bytes(ebuf.at[pl.ds(0, GRP - 1)], e_send)
    wait_bytes(dbuf.at[pl.ds(1, DP - 1)], d_send)
    for l in range(DECODER_LAYERS):
        for kind in range(2):
            buf = (wqx, wox)[kind]
            wait_bytes(buf.at[l, pl.ds(0, SLICES - 1), half, :], w_send.at[l, kind])
            wait_bytes(buf.at[l, :, half, :], f_send.at[l, kind])
        wait_bytes(p1r.at[l, pl.ds(0, SLICES - 1)], p1_send.at[l])
        wait_bytes(p2r.at[l, pl.ds(1, PLANES - 1)], p2_send.at[l])
        wait_bytes(p3r.at[l, pl.ds(0, PLANES - 1)], p3_send.at[l])
    wait_bytes(p4r.at[pl.ds(1, SLICES - 1)], p4_send.at[0])
    own_last = t // 2 == z

    @pl.when(own_last)
    def _():
        wait_bytes(pfr.at[pl.ds(0, SLICES - 1)], p4_send.at[1])

    @pl.when(jnp.logical_not(own_last))
    def _():
        wait_bytes(pfr, p4_send.at[1])


def decode(rows, idx, extra, gain, cosine, sine, lengths, wq, wo, cache):
    vmem = pl.BlockSpec(memory_space=pltpu.VMEM)
    hbm = pl.BlockSpec(memory_space=pl.ANY)
    layers = DECODER_LAYERS
    dma = pltpu.SemaphoreType.DMA
    return pl.pallas_call(
        main_kernel,
        out_shape=jax.ShapeDtypeStruct((TOKENS, 512), BF),
        in_specs=[
            vmem,
            vmem,
            vmem,
            vmem,
            vmem,
            vmem,
            pl.BlockSpec(memory_space=pltpu.SMEM),
            hbm,
            hbm,
            hbm,
        ],
        out_specs=vmem,
        scratch_shapes=[
            pltpu.VMEM((layers, REPLICA_ROWS, CACHE, 2 * D), BF),
            pltpu.VMEM((layers, SLICES, D, QKV), BF),
            pltpu.VMEM((layers, SLICES, D, 512), BF),
            pltpu.VMEM((GRP, SLOTS, D), BF),
            pltpu.VMEM((DP, ALL, D), BF),
            pltpu.VMEM((DP, ALL, D), BF),
            pltpu.VMEM((ALL, D), F32),
            pltpu.VMEM((layers, ALL + 16, D), BF),
            pltpu.VMEM((layers, SLICES, ALL + 16, D), BF),
            pltpu.VMEM((layers, PLANES, 208, D), BF),
            pltpu.VMEM((layers, PLANES, 208, D), BF),
            pltpu.VMEM((4 * TOKENS, D), F32),
            pltpu.VMEM((2, 16 * REPLICA_ROWS, D), F32),
            pltpu.VMEM((4 * TOKENS, D), F32),
            pltpu.VMEM((layers, 4 * TOKENS, D), BF),
            pltpu.VMEM((layers, PLANES, 4 * TOKENS, D), BF),
            pltpu.VMEM((SLICES, ALL, D), BF),
            pltpu.VMEM((SLICES, ALL, D), BF),
            pltpu.VMEM((PLANES, 2, TOKENS, 512), BF),
            pltpu.VMEM((SLICES, TOKENS, 512), BF),
            dma((layers,)),
            dma((layers, 2)),
            dma((layers, 2)),
            dma((layers, 2)),
            dma((layers, 2)),
            dma,
            dma,
            dma,
            dma,
            dma((layers,)),
            dma((layers,)),
            dma((layers,)),
            dma((layers,)),
            dma((layers,)),
            dma((layers,)),
            dma((2,)),
            dma((2,)),
        ],
        compiler_params=pltpu.CompilerParams(
            collective_id=1, has_side_effects=True, vmem_limit_bytes=40 * 1024 * 1024
        ),
        name="decode",
    )(rows, idx, extra, gain, cosine, sine, lengths, wq, wo, cache)


def body(
    token_ids,
    start_pos,
    cache_len,
    embed_table,
    norm_gain,
    query_key_value_weight,
    output_weight,
    key_value_cache,
):
    a, g = lax.axis_index("dp"), lax.axis_index("grp")
    z = g // SLICES
    me = a * GRP + g
    shard_rows = embed_table.shape[0]
    number = DP * ALL

    ids = gather_ids(token_ids[0].transpose(0, 2, 1).reshape(ALL))[:, 0, :].reshape(number)
    owner = ids // shard_rows
    order = jnp.arange(number, dtype=jnp.int32)
    same_id = ids[:, None] == ids[None, :]
    first = jnp.min(jnp.where(same_id, order[None, :], number), axis=1)
    is_first = first == order
    before = is_first[None, :] & (owner[:, None] == owner[None, :]) & (order[None, :] < first[:, None])
    slot = jnp.sum(before.astype(jnp.int32), axis=1)
    holds = (
        is_first[None, :]
        & (owner[None, :] == me)
        & (slot[None, :] == jnp.arange(SLOTS, dtype=jnp.int32)[:, None])
    )
    local = jnp.sum(jnp.where(holds, ids[None, :] - me * shard_rows, 0), axis=1)
    rows = jnp.take(embed_table, local, axis=0, mode="clip")
    rows = rows.reshape(SLOTS, GRP, D).transpose(1, 0, 2)
    idx = jnp.where((owner // GRP == a) & (slot < SLOTS), (owner % GRP) * SLOTS + slot, -1)

    def overflow(_):
        late = (owner == me) & (slot >= SLOTS)
        more = jnp.take(embed_table, jnp.where(late, ids - me * shard_rows, 0), axis=0, mode="clip")
        more = jnp.where(late[:, None], more.astype(F32), 0.0).reshape(DP, ALL, GRP, D)
        more = lax.psum_scatter(more, "dp", scatter_dimension=0, tiled=False)
        return lax.psum_scatter(more, "grp", scatter_dimension=1, tiled=False)

    extra = lax.cond(
        jnp.max(slot) >= SLOTS, overflow, lambda _: jnp.zeros((ALL, D), F32), jnp.int32(0)
    )

    lengths = lax.dynamic_index_in_dim(cache_len[0], z, 0, keepdims=False)
    starts = lax.dynamic_index_in_dim(start_pos[0], z, 0, keepdims=False)
    position = (starts[None, :] + jnp.arange(DECODE_STEPS, dtype=jnp.int32)[:, None]).reshape(TOKENS)
    exponent = jnp.arange(HEAD_SIZE // 2, dtype=F32) * (2.0 / HEAD_SIZE)
    frequency = jnp.power(F32(ROPE_BASE), -exponent)
    angles = position.astype(F32)[:, None] * frequency
    cosine, sine = jnp.cos(angles), jnp.sin(angles)
    cosine = jnp.concatenate([cosine, cosine], axis=1)
    sine = jnp.concatenate([-sine, sine], axis=1)
    gain = lax.dynamic_slice_in_dim(norm_gain, g * D, D, 1).reshape(DECODER_LAYERS, 1, D)

    out = decode(
        rows,
        idx.reshape(number, 1),
        extra,
        gain,
        cosine,
        sine,
        lengths,
        query_key_value_weight,
        output_weight,
        key_value_cache.reshape(DECODER_LAYERS, REPLICA_ROWS, CACHE, 2 * D),
    )
    return out.reshape(DECODE_STEPS, REPLICA_ROWS, 512).transpose(1, 0, 2)[:, None]


def solution(mesh):
    return jax.shard_map(
        body,
        mesh=mesh,
        in_specs=(
            P("dp", None, None, None),
            P("dp", None, None),
            P("dp", None, None),
            P(("dp", "grp"), None),
            P(),
            P(None, "grp", None),
            P(None, "grp", None),
            P(None, "dp", "grp", None, None),
        ),
        out_specs=P("dp", "grp", None, None),
        check_vma=False,
    )
```

```python
import jax
import jax.numpy as jnp
from jax import lax
from jax.experimental import pallas as pl
from jax.experimental.pallas import tpu as pltpu
from jax.sharding import PartitionSpec as P

MODEL_WIDTH = 4096
QUERY_HEADS = 32
KEY_VALUE_HEADS = 8
HEAD_SIZE = 128
DECODER_LAYERS = 2
DECODE_STEPS = 4
REPLICA_ROWS = 8
ROPE_BASE = 500000.0
EPSILON = 1e-05

MESH = pl.DeviceIdType.MESH
SLOTS = 16
DP = 4
PLANES = 4
SLICES = 8
GRP = PLANES * SLICES
TOKENS = REPLICA_ROWS * DECODE_STEPS
ALL = PLANES * TOKENS
D = 128
QKV = 768
CACHE = 1024
FRESH_AT = CACHE - DECODE_STEPS
BF = jnp.bfloat16
F32 = jnp.float32


def ids_kernel(ids_ref, out_ref, land, send_sem, recv_sem):
    a, g = lax.axis_index("dp"), lax.axis_index("grp")
    barrier = pltpu.get_barrier_semaphore()
    for j in range(1, DP):
        pl.semaphore_signal(barrier, inc=1, device_id=((a + j) % DP, g), device_id_type=MESH)
    pl.semaphore_wait(barrier, DP - 1)
    copies = []
    for j in range(1, DP):
        copy = pltpu.make_async_remote_copy(
            src_ref=ids_ref,
            dst_ref=land.at[j],
            send_sem=send_sem.at[j],
            recv_sem=recv_sem.at[j],
            device_id=((a + j) % DP, g),
            device_id_type=MESH,
        )
        copy.start()
        copies.append(copy)
    out_ref[a] = ids_ref[...]
    for j in range(1, DP):
        copies[j - 1].wait()
        out_ref[(a - j + DP) % DP] = land[j]


def gather_ids(ids):
    return pl.pallas_call(
        ids_kernel,
        out_shape=jax.ShapeDtypeStruct((DP, 8, ALL), jnp.int32),
        in_specs=[pl.BlockSpec(memory_space=pltpu.VMEM)],
        out_specs=pl.BlockSpec(memory_space=pltpu.VMEM),
        scratch_shapes=[
            pltpu.VMEM((DP, 8, ALL), jnp.int32),
            pltpu.SemaphoreType.DMA((DP,)),
            pltpu.SemaphoreType.DMA((DP,)),
        ],
        compiler_params=pltpu.CompilerParams(collective_id=0, has_side_effects=True),
        name="gather_ids",
    )(jnp.broadcast_to(ids[None], (8, ALL)))


def main_kernel(
    rows_ref,
    idx_ref,
    extra_ref,
    gain_ref,
    cos_ref,
    sin_ref,
    len_ref,
    wq_ref,
    wo_ref,
    cache_ref,
    out_ref,
    cache_v,
    wqx,
    wox,
    ebuf,
    tbuf,
    dbuf,
    stream,
    p1s,
    p1r,
    p2s,
    p2r,
    qs,
    kvs,
    atts,
    p3s,
    p3r,
    p4s,
    p4r,
    last,
    final,
    cache_sem,
    w_send,
    w_recv,
    f_send,
    f_recv,
    e_send,
    e_recv,
    d_send,
    d_recv,
    p1_send,
    p1_recv,
    p2_send,
    p2_recv,
    p3_send,
    p3_recv,
    p4_send,
    p4_recv,
    o_send,
    o_recv,
):
    a, g = lax.axis_index("dp"), lax.axis_index("grp")
    core = a % 2
    sibling = a + 1 - 2 * core
    z, t = g // SLICES, g % SLICES
    y, x = t // 4, t % 4

    def remote(src, dst, send_sem, recv_sem, a2, g2):
        return pltpu.make_async_remote_copy(
            src_ref=src,
            dst_ref=dst,
            send_sem=send_sem,
            recv_sem=recv_sem,
            device_id=(a2, g2),
            device_id_type=MESH,
        )

    def wait_bytes(ref, sem):
        pltpu.make_async_copy(ref, ref, sem).wait()

    def slice_at(j):
        return ((y + j // 4) % 2) * 4 + (x + j % 4) % 4

    for l in range(DECODER_LAYERS):
        pltpu.make_async_copy(cache_ref.at[l], cache_v.at[l], cache_sem.at[l]).start()

    barrier = pltpu.get_barrier_semaphore()

    def greet(j, c):
        pl.semaphore_signal(barrier, inc=1, device_id=(a, (g + j) % GRP), device_id_type=MESH)
        return c

    lax.fori_loop(1, GRP, greet, 0)
    for j in range(1, DP):
        pl.semaphore_signal(barrier, inc=1, device_id=((a + j) % DP, g), device_id_type=MESH)
    pl.semaphore_wait(barrier, GRP - 1 + DP - 1)

    def send_rows(j, c):
        g2 = ((z + j // SLICES) % PLANES) * SLICES + slice_at(j % SLICES)
        remote(rows_ref.at[g2], ebuf.at[g], e_send, e_recv, a, g2).start()
        return c

    lax.fori_loop(1, GRP, send_rows, 0)

    half = pl.ds(pl.multiple_of(core * 64, 64), 64)

    def qkv_pieces(l, t2):
        return (
            (
                wq_ref.at[l, half, pl.ds(pl.multiple_of(t2 * 512, 512), 512)],
                wqx.at[l, t, half, pl.ds(0, 512)],
            ),
            (
                wq_ref.at[l, half, pl.ds(pl.multiple_of(4096 + t2 * 128, 128), 128)],
                wqx.at[l, t, half, pl.ds(512, 128)],
            ),
            (
                wq_ref.at[l, half, pl.ds(pl.multiple_of(5120 + t2 * 128, 128), 128)],
                wqx.at[l, t, half, pl.ds(640, 128)],
            ),
        )

    def out_pieces(l, t2):
        return (
            (
                wo_ref.at[l, half, pl.ds(pl.multiple_of(t2 * 512, 512), 512)],
                wox.at[l, t, half, :],
            ),
        )

    def send_weights(l, kind):
        pieces = (qkv_pieces, out_pieces)[kind]

        def one(j, c):
            t2 = slice_at(j)
            for src, dst in pieces(l, t2):
                remote(src, dst, w_send.at[l, kind], w_recv.at[l, kind], a, z * SLICES + t2).start()
            return c

        lax.fori_loop(1, SLICES, one, 0)
        for src, dst in pieces(l, t):
            pltpu.make_async_copy(src, dst, w_recv.at[l, kind]).start()

    def forward_weights(l, kind):
        buf = (wqx, wox)[kind]
        wait_bytes(buf.at[l, :, half, :], w_recv.at[l, kind])
        remote(
            buf.at[l, :, half, :],
            buf.at[l, :, half, :],
            f_send.at[l, kind],
            f_recv.at[l, kind],
            sibling,
            g,
        ).start()

    def await_weights(l, kind):
        buf = (wqx, wox)[kind]
        wait_bytes(buf.at[l, :, half, :], f_recv.at[l, kind])

    send_weights(0, 0)
    ebuf[g] = rows_ref[g]
    kvs[...] = jnp.zeros_like(kvs)
    wait_bytes(ebuf.at[pl.ds(0, GRP - 1)], e_recv)
    table = ebuf[...].reshape(GRP * SLOTS, D)

    def picked(a2):
        want = idx_ref[pl.ds(pl.multiple_of(a2 * ALL, ALL), ALL), :]
        place = lax.broadcasted_iota(jnp.int32, (ALL, GRP * SLOTS), 1)
        chosen = jnp.where(place == want, 1.0, 0.0).astype(BF)
        return jnp.dot(chosen, table, preferred_element_type=F32)

    for j in range(1, DP):
        a2 = (a + j) % DP
        tbuf[j] = picked(a2).astype(BF)
        remote(tbuf.at[j], dbuf.at[j], d_send, d_recv, a2, g).start()
    send_weights(0, 1)
    mine = picked(a) + extra_ref[...]
    wait_bytes(dbuf.at[pl.ds(1, DP - 1)], d_recv)
    for j in range(1, DP):
        mine = mine + dbuf[j].astype(F32)
    stream[...] = mine

    row32 = lax.broadcasted_iota(jnp.int32, (TOKENS, ALL), 0)
    lane32 = lax.broadcasted_iota(jnp.int32, (TOKENS, ALL), 1)
    own_token = lane32 == row32 + z * TOKENS

    def split(value):
        high = value.astype(BF).astype(F32)
        return jnp.concatenate([high, value - high], axis=0).astype(BF)

    for l in range(DECODER_LAYERS):
        s = stream[...]
        square = s * s
        high = square.astype(BF)
        low = (square - high.astype(F32)).astype(BF)
        ones = jnp.ones((8, D), BF)
        contract = (((1,), (1,)), ((), ()))
        sums = lax.dot_general(ones, high, contract, preferred_element_type=F32)
        sums = sums + lax.dot_general(ones, low, contract, preferred_element_type=F32)
        p1s[l, 0:ALL, :] = (s * gain_ref[l]).astype(BF)
        p1s[l, ALL : ALL + 16, :] = split(sums)

        def send_stream(j, c):
            remote(
                p1s.at[l], p1r.at[l, t], p1_send.at[l], p1_recv.at[l], a, z * SLICES + slice_at(j)
            ).start()
            return c

        lax.fori_loop(1, SLICES, send_stream, 0)
        p1r[l, t] = p1s[l]
        forward_weights(l, 0)
        wait_bytes(p1r.at[l, pl.ds(0, SLICES - 1)], p1_recv.at[l])
        await_weights(l, 0)

        left = jnp.concatenate([p1r[l, j, 0:ALL, :] for j in range(SLICES)], axis=1)
        sums = jnp.zeros((8, ALL), F32)
        for j in range(SLICES):
            tile = p1r[l, j, ALL : ALL + 16, :].astype(F32)
            sums = sums + tile[0:8] + tile[8:16]
        projected = jnp.dot(
            left, wqx[l].reshape(SLICES * D, QKV), preferred_element_type=F32
        ).astype(BF)
        sums = split(sums)
        for r in range(PLANES):
            for c in range(QKV // D):
                p2s[l, r, c * TOKENS : (c + 1) * TOKENS, :] = projected[
                    r * TOKENS : (r + 1) * TOKENS, c * D : (c + 1) * D
                ]
            p2s[l, r, 192:208, :] = sums
        for j in range(1, PLANES):
            z2 = (z + j) % PLANES
            remote(
                p2s.at[l, z2], p2r.at[l, j], p2_send.at[l], p2_recv.at[l], a, z2 * SLICES + t
            ).start()
        forward_weights(l, 1)
        wait_bytes(p2r.at[l, pl.ds(1, PLANES - 1)], p2_recv.at[l])
        if l + 1 < DECODER_LAYERS:
            send_weights(l + 1, 0)
        total = p2s[l, z].astype(F32)
        for j in range(1, PLANES):
            total = total + p2r[l, j].astype(F32)

        line = total[192:193] + total[200:201]
        column = jnp.sum(
            jnp.where(own_token, jnp.broadcast_to(line, (TOKENS, ALL)), 0.0), axis=1, keepdims=True
        )
        factor = lax.rsqrt(column * (1.0 / MODEL_WIDTH) + EPSILON)
        cosine, sine = cos_ref[...], sin_ref[...]

        def rotated(block):
            return block * cosine + pltpu.roll(block, 64, 1) * sine

        for h in range(4):
            qs[h * TOKENS : (h + 1) * TOKENS, :] = rotated(
                total[h * TOKENS : (h + 1) * TOKENS] * factor
            )
        kvs[0, 96:128, :] = rotated(total[128:160] * factor)
        kvs[1, 96:128, :] = total[160:192] * factor
        pltpu.make_async_copy(cache_ref.at[l], cache_v.at[l], cache_sem.at[l]).wait()
        fresh_row = lax.broadcasted_iota(jnp.int32, (16, D), 0) >= 12
        place = lax.broadcasted_iota(jnp.int32, (16, CACHE), 1)
        step = lax.broadcasted_iota(jnp.int32, (16, CACHE), 0) % DECODE_STEPS
        fresh_live = (place >= FRESH_AT) & (place - FRESH_AT <= step)
        for b in range(REPLICA_ROWS):
            for k in range(2):
                old = cache_v[l, b, CACHE - 16 : CACHE, k * D : (k + 1) * D].astype(F32)
                new = kvs[k, pl.ds(b, 16, stride=8), :]
                cache_v[l, b, CACHE - 16 : CACHE, k * D : (k + 1) * D] = jnp.where(
                    fresh_row, new, old
                ).astype(BF)
        for b in range(REPLICA_ROWS):
            query = qs[pl.ds(b, 16, stride=8), :].astype(BF)
            scores = lax.dot_general(
                query, cache_v[l, b, :, 0:D], contract, preferred_element_type=F32
            ) * (HEAD_SIZE**-0.5)
            live = (place < len_ref[b]) | fresh_live
            scores = jnp.where(live, scores, -1e30)
            top = jnp.max(scores, axis=1, keepdims=True)
            power = jnp.exp(scores - top)
            whole = jnp.sum(power, axis=1, keepdims=True)
            value = jnp.dot(power.astype(BF), cache_v[l, b, :, D : 2 * D], preferred_element_type=F32)
            atts[pl.ds(b, 16, stride=8), :] = value / whole

        p3s[l] = atts[...].astype(BF)
        for j in range(1, PLANES):
            z2 = (z + j) % PLANES
            remote(
                p3s.at[l], p3r.at[l, z], p3_send.at[l], p3_recv.at[l], a, z2 * SLICES + t
            ).start()
        p3r[l, z] = p3s[l]
        await_weights(l, 1)
        wait_bytes(p3r.at[l, pl.ds(0, PLANES - 1)], p3_recv.at[l])
        if l + 1 < DECODER_LAYERS:
            send_weights(l + 1, 1)
        left = jnp.concatenate(
            [
                jnp.concatenate(
                    [p3r[l, r, h * TOKENS : (h + 1) * TOKENS, :] for r in range(PLANES)], axis=0
                )
                for h in range(4)
            ],
            axis=1,
        )

        def partial(t2):
            return lax.dot_general(left, wox[l, t2], contract, preferred_element_type=F32)

        for j in range(1, SLICES):
            t2 = slice_at(j)
            p4s[l, j] = partial(t2).astype(BF)
            remote(
                p4s.at[l, j], p4r.at[l, j], p4_send.at[l], p4_recv.at[l], a, z * SLICES + t2
            ).start()
        s = stream[...] + partial(t)
        wait_bytes(p4r.at[l, pl.ds(1, SLICES - 1)], p4_recv.at[l])
        for j in range(1, SLICES):
            s = s + p4r[l, j].astype(F32)
        stream[...] = s

    last[...] = stream[...].astype(BF)
    home = g // 4
    for j in range(PLANES):
        r = (z + j) % PLANES
        g2 = r * SLICES + home
        tokens = last.at[pl.ds(pl.multiple_of(r * TOKENS, TOKENS), TOKENS), :]

        @pl.when(g2 != g)
        def _():
            remote(tokens, final.at[g % 4], o_send, o_recv, a, g2).start()

        @pl.when(g2 == g)
        def _():
            pltpu.make_async_copy(tokens, final.at[g % 4], o_recv).start()

    wait_bytes(final, o_recv)
    for k in range(4):
        out_ref[:, k * D : (k + 1) * D] = final[k]

    wait_bytes(ebuf.at[pl.ds(0, GRP - 1)], e_send)
    wait_bytes(dbuf.at[pl.ds(1, DP - 1)], d_send)
    for l in range(DECODER_LAYERS):
        for kind in range(2):
            buf = (wqx, wox)[kind]
            wait_bytes(buf.at[l, pl.ds(0, SLICES - 1), half, :], w_send.at[l, kind])
            wait_bytes(buf.at[l, :, half, :], f_send.at[l, kind])
        wait_bytes(p1r.at[l, pl.ds(0, SLICES - 1)], p1_send.at[l])
        wait_bytes(p2r.at[l, pl.ds(1, PLANES - 1)], p2_send.at[l])
        wait_bytes(p3r.at[l, pl.ds(0, PLANES - 1)], p3_send.at[l])
        wait_bytes(p4r.at[l, pl.ds(1, SLICES - 1)], p4_send.at[l])

    @pl.when(home == t)
    def _():
        wait_bytes(final.at[pl.ds(0, PLANES - 1)], o_send)

    @pl.when(home != t)
    def _():
        wait_bytes(final, o_send)


def decode(rows, idx, extra, gain, cosine, sine, lengths, wq, wo, cache):
    vmem = pl.BlockSpec(memory_space=pltpu.VMEM)
    hbm = pl.BlockSpec(memory_space=pl.ANY)
    layers = DECODER_LAYERS
    dma = pltpu.SemaphoreType.DMA
    return pl.pallas_call(
        main_kernel,
        out_shape=jax.ShapeDtypeStruct((TOKENS, 512), BF),
        in_specs=[
            vmem,
            vmem,
            vmem,
            vmem,
            vmem,
            vmem,
            pl.BlockSpec(memory_space=pltpu.SMEM),
            hbm,
            hbm,
            hbm,
        ],
        out_specs=vmem,
        scratch_shapes=[
            pltpu.VMEM((layers, REPLICA_ROWS, CACHE, 2 * D), BF),
            pltpu.VMEM((layers, SLICES, D, QKV), BF),
            pltpu.VMEM((layers, SLICES, D, 512), BF),
            pltpu.VMEM((GRP, SLOTS, D), BF),
            pltpu.VMEM((DP, ALL, D), BF),
            pltpu.VMEM((DP, ALL, D), BF),
            pltpu.VMEM((ALL, D), F32),
            pltpu.VMEM((layers, ALL + 16, D), BF),
            pltpu.VMEM((layers, SLICES, ALL + 16, D), BF),
            pltpu.VMEM((layers, PLANES, 208, D), BF),
            pltpu.VMEM((layers, PLANES, 208, D), BF),
            pltpu.VMEM((4 * TOKENS, D), F32),
            pltpu.VMEM((2, 16 * REPLICA_ROWS, D), F32),
            pltpu.VMEM((4 * TOKENS, D), F32),
            pltpu.VMEM((layers, 4 * TOKENS, D), BF),
            pltpu.VMEM((layers, PLANES, 4 * TOKENS, D), BF),
            pltpu.VMEM((layers, SLICES, ALL, D), BF),
            pltpu.VMEM((layers, SLICES, ALL, D), BF),
            pltpu.VMEM((ALL, D), BF),
            pltpu.VMEM((4, TOKENS, D), BF),
            dma((layers,)),
            dma((layers, 2)),
            dma((layers, 2)),
            dma((layers, 2)),
            dma((layers, 2)),
            dma,
            dma,
            dma,
            dma,
            dma((layers,)),
            dma((layers,)),
            dma((layers,)),
            dma((layers,)),
            dma((layers,)),
            dma((layers,)),
            dma((layers,)),
            dma((layers,)),
            dma,
            dma,
        ],
        compiler_params=pltpu.CompilerParams(
            collective_id=1, has_side_effects=True, vmem_limit_bytes=40 * 1024 * 1024
        ),
        name="decode",
    )(rows, idx, extra, gain, cosine, sine, lengths, wq, wo, cache)


def body(
    token_ids,
    start_pos,
    cache_len,
    embed_table,
    norm_gain,
    query_key_value_weight,
    output_weight,
    key_value_cache,
):
    a, g = lax.axis_index("dp"), lax.axis_index("grp")
    z = g // SLICES
    me = a * GRP + g
    shard_rows = embed_table.shape[0]
    number = DP * ALL

    ids = gather_ids(token_ids[0].transpose(0, 2, 1).reshape(ALL))[:, 0, :].reshape(number)
    owner = ids // shard_rows
    order = jnp.arange(number, dtype=jnp.int32)
    same_id = ids[:, None] == ids[None, :]
    first = jnp.min(jnp.where(same_id, order[None, :], number), axis=1)
    is_first = first == order
    before = is_first[None, :] & (owner[:, None] == owner[None, :]) & (order[None, :] < first[:, None])
    slot = jnp.sum(before.astype(jnp.int32), axis=1)
    holds = (
        is_first[None, :]
        & (owner[None, :] == me)
        & (slot[None, :] == jnp.arange(SLOTS, dtype=jnp.int32)[:, None])
    )
    local = jnp.sum(jnp.where(holds, ids[None, :] - me * shard_rows, 0), axis=1)
    rows = jnp.take(embed_table, local, axis=0, mode="clip")
    rows = rows.reshape(SLOTS, GRP, D).transpose(1, 0, 2)
    idx = jnp.where((owner // GRP == a) & (slot < SLOTS), (owner % GRP) * SLOTS + slot, -1)

    def overflow(_):
        late = (owner == me) & (slot >= SLOTS)
        more = jnp.take(embed_table, jnp.where(late, ids - me * shard_rows, 0), axis=0, mode="clip")
        more = jnp.where(late[:, None], more, jnp.zeros_like(more)).reshape(DP, ALL, GRP, D)
        more = more.transpose(0, 2, 1, 3).reshape(DP * GRP, ALL, D)
        more = lax.all_to_all(more, ("dp", "grp"), split_axis=0, concat_axis=0, tiled=True)
        return jnp.sum(more.astype(F32), axis=0)

    extra = lax.cond(
        jnp.max(slot) >= SLOTS, overflow, lambda _: jnp.zeros((ALL, D), F32), jnp.int32(0)
    )

    lengths = lax.dynamic_index_in_dim(cache_len[0], z, 0, keepdims=False)
    starts = lax.dynamic_index_in_dim(start_pos[0], z, 0, keepdims=False)
    position = (starts[None, :] + jnp.arange(DECODE_STEPS, dtype=jnp.int32)[:, None]).reshape(TOKENS)
    exponent = jnp.arange(HEAD_SIZE // 2, dtype=F32) * (2.0 / HEAD_SIZE)
    frequency = jnp.power(F32(ROPE_BASE), -exponent)
    angles = position.astype(F32)[:, None] * frequency
    cosine, sine = jnp.cos(angles), jnp.sin(angles)
    cosine = jnp.concatenate([cosine, cosine], axis=1)
    sine = jnp.concatenate([-sine, sine], axis=1)
    gain = lax.dynamic_slice_in_dim(norm_gain, g * D, D, 1).reshape(DECODER_LAYERS, 1, D)

    out = decode(
        rows,
        idx.reshape(number, 1),
        extra,
        gain,
        cosine,
        sine,
        lengths,
        query_key_value_weight,
        output_weight,
        key_value_cache.reshape(DECODER_LAYERS, REPLICA_ROWS, CACHE, 2 * D),
    )
    return out.reshape(DECODE_STEPS, REPLICA_ROWS, 512).transpose(1, 0, 2)[:, None]


def solution(mesh):
    return jax.shard_map(
        body,
        mesh=mesh,
        in_specs=(
            P("dp", None, None, None),
            P("dp", None, None),
            P("dp", None, None),
            P(("dp", "grp"), None),
            P(),
            P(None, "grp", None),
            P(None, "grp", None),
            P(None, "dp", "grp", None, None),
        ),
        out_specs=P("dp", "grp", None, None),
        check_vma=False,
    )
```

```python
import jax
import jax.numpy as jnp
from jax import lax
from jax.experimental import pallas as pl
from jax.experimental.pallas import tpu as pltpu
from jax.sharding import PartitionSpec as P

MODEL_WIDTH = 4096
QUERY_HEADS = 32
KEY_VALUE_HEADS = 8
HEAD_SIZE = 128
DECODER_LAYERS = 2
DECODE_STEPS = 4
REPLICA_ROWS = 8
ROPE_BASE = 500000.0
EPSILON = 1e-05

MESH = pl.DeviceIdType.MESH
SLOTS = 16
DP = 4
PLANES = 4
SLICES = 8
GRP = PLANES * SLICES
TOKENS = REPLICA_ROWS * DECODE_STEPS
ALL = PLANES * TOKENS
D = 128
QKV = 768
CACHE = 1024
SHARD = 1002
SHARD_WHOLE = 992
FRESH_AT = CACHE - DECODE_STEPS
BF = jnp.bfloat16
F32 = jnp.float32


def main_kernel(
    ids_ref,
    extra_ref,
    gain_ref,
    cos_ref,
    sin_ref,
    len_ref,
    wq_ref,
    wo_ref,
    cache_ref,
    embed_ref,
    out_ref,
    all_ref,
    most_ref,
    cache_v,
    shard_v,
    land,
    tail_v,
    rows_v,
    chosen_v,
    wqx,
    wox,
    ebuf,
    tbuf,
    dbuf,
    stream,
    p1s,
    p1r,
    p2s,
    p2r,
    qs,
    kvs,
    atts,
    p3s,
    p3r,
    p4s,
    p4r,
    last,
    final,
    cache_sem,
    w_send,
    w_recv,
    f_send,
    f_recv,
    e_send,
    e_recv,
    d_send,
    d_recv,
    p1_send,
    p1_recv,
    p2_send,
    p2_recv,
    p3_send,
    p3_recv,
    p4_send,
    p4_recv,
    o_send,
    o_recv,
    i_send,
    i_recv,
    s_sem,
):
    a, g = lax.axis_index("dp"), lax.axis_index("grp")
    core = a % 2
    sibling = a + 1 - 2 * core
    z, t = g // SLICES, g % SLICES
    y, x = t // 4, t % 4

    def remote(src, dst, send_sem, recv_sem, a2, g2):
        return pltpu.make_async_remote_copy(
            src_ref=src,
            dst_ref=dst,
            send_sem=send_sem,
            recv_sem=recv_sem,
            device_id=(a2, g2),
            device_id_type=MESH,
        )

    def wait_bytes(ref, sem):
        pltpu.make_async_copy(ref, ref, sem).wait()

    def slice_at(j):
        return ((y + j // 4) % 2) * 4 + (x + j % 4) % 4

    shard_copy = pltpu.make_async_copy(embed_ref, shard_v, s_sem)
    shard_copy.start()
    for l in range(DECODER_LAYERS):
        pltpu.make_async_copy(cache_ref.at[l], cache_v.at[l], cache_sem.at[l]).start()

    barrier = pltpu.get_barrier_semaphore()

    def greet(j, c):
        pl.semaphore_signal(barrier, inc=1, device_id=(a, (g + j) % GRP), device_id_type=MESH)
        return c

    lax.fori_loop(1, GRP, greet, 0)
    for j in range(1, DP):
        pl.semaphore_signal(barrier, inc=1, device_id=((a + j) % DP, g), device_id_type=MESH)
    pl.semaphore_wait(barrier, GRP - 1 + DP - 1)

    land[a] = ids_ref[...]
    for j in range(1, DP):
        remote(ids_ref, land.at[a], i_send, i_recv, (a + j) % DP, g).start()

    half = pl.ds(pl.multiple_of(core * 64, 64), 64)

    def qkv_pieces(l, t2):
        return (
            (
                wq_ref.at[l, half, pl.ds(pl.multiple_of(t2 * 512, 512), 512)],
                wqx.at[l, t, half, pl.ds(0, 512)],
            ),
            (
                wq_ref.at[l, half, pl.ds(pl.multiple_of(4096 + t2 * 128, 128), 128)],
                wqx.at[l, t, half, pl.ds(512, 128)],
            ),
            (
                wq_ref.at[l, half, pl.ds(pl.multiple_of(5120 + t2 * 128, 128), 128)],
                wqx.at[l, t, half, pl.ds(640, 128)],
            ),
        )

    def out_pieces(l, t2):
        return (
            (
                wo_ref.at[l, half, pl.ds(pl.multiple_of(t2 * 512, 512), 512)],
                wox.at[l, t, half, :],
            ),
        )

    def send_weights(l, kind):
        pieces = (qkv_pieces, out_pieces)[kind]

        def one(j, c):
            t2 = slice_at(j)
            for src, dst in pieces(l, t2):
                remote(src, dst, w_send.at[l, kind], w_recv.at[l, kind], a, z * SLICES + t2).start()
            return c

        lax.fori_loop(1, SLICES, one, 0)
        for src, dst in pieces(l, t):
            pltpu.make_async_copy(src, dst, w_recv.at[l, kind]).start()

    def forward_weights(l, kind):
        buf = (wqx, wox)[kind]
        wait_bytes(buf.at[l, :, half, :], w_recv.at[l, kind])
        remote(
            buf.at[l, :, half, :],
            buf.at[l, :, half, :],
            f_send.at[l, kind],
            f_recv.at[l, kind],
            sibling,
            g,
        ).start()

    def await_weights(l, kind):
        buf = (wqx, wox)[kind]
        wait_bytes(buf.at[l, :, half, :], f_recv.at[l, kind])

    send_weights(0, 0)
    send_weights(0, 1)
    kvs[...] = jnp.zeros_like(kvs)
    wait_bytes(land.at[pl.ds(0, DP - 1)], i_recv)

    number = DP * ALL
    all_ref[...] = land[...]
    along = jnp.concatenate([land[k] for k in range(DP)], axis=1).astype(F32)
    line_of = lax.broadcasted_iota(jnp.int32, (1, number), 1).astype(F32)
    line_id = along[0:1]
    columns = []
    for k in range(DP):
        square = jnp.concatenate([along[:, k * ALL : (k + 1) * ALL]] * 16, axis=0)
        columns.append(jnp.transpose(square)[:, 0:1])

    def owner_of(ids):
        return jnp.floor((ids + 0.5) * (1.0 / SHARD))

    first_line = jnp.full((1, number), float(number), F32)
    first_column = []
    for k in range(DP):
        same = columns[k] == line_id
        up = lax.broadcasted_iota(jnp.int32, (ALL, number), 0).astype(F32) + float(k * ALL)
        first_line = jnp.minimum(
            first_line, jnp.min(jnp.where(same, up, float(number)), axis=0, keepdims=True)
        )
        first_column.append(jnp.min(jnp.where(same, line_of, float(number)), axis=1, keepdims=True))
    is_first = first_line == line_of
    line_owner = owner_of(line_id)
    me = (a * GRP + g).astype(F32)

    held = jnp.where(is_first & (line_owner == me), 1.0, 0.0)
    earlier = lax.broadcasted_iota(jnp.int32, (number, number), 0) < lax.broadcasted_iota(
        jnp.int32, (number, number), 1
    )
    earlier = jnp.where(earlier, 1.0, 0.0).astype(BF)
    rank = jnp.dot(
        jnp.broadcast_to(held, (8, number)).astype(BF), earlier, preferred_element_type=F32
    )[0:1]
    slot_no = lax.broadcasted_iota(jnp.int32, (SLOTS, number), 0).astype(F32)
    local = jnp.sum(
        jnp.where((held > 0.0) & (rank == slot_no), line_id - me * float(SHARD), 0.0),
        axis=1,
        keepdims=True,
    )
    entry = lax.broadcasted_iota(jnp.int32, (SLOTS, SHARD_WHOLE), 1).astype(F32)
    take = jnp.where(entry == local, 1.0, 0.0).astype(BF)
    tail = lax.broadcasted_iota(jnp.int32, (SLOTS, 16), 1).astype(F32) + float(SHARD_WHOLE)
    take_tail = jnp.where(tail == local, 1.0, 0.0).astype(BF)
    shard_copy.wait()
    tail_v[...] = jnp.zeros_like(tail_v)
    tail_v[0 : SHARD - SHARD_WHOLE, :] = shard_v[SHARD_WHOLE:SHARD, :]
    rows = jnp.dot(take, shard_v[0:SHARD_WHOLE, :], preferred_element_type=F32)
    rows = rows + jnp.dot(take_tail, tail_v[...], preferred_element_type=F32)
    rows = rows.astype(BF)
    for k in range(GRP):
        rows_v[k] = rows[:, k * D : (k + 1) * D]

    def send_rows(j, c):
        g2 = ((z + j // SLICES) % PLANES) * SLICES + slice_at(j % SLICES)
        remote(rows_v.at[g2], ebuf.at[g], e_send, e_recv, a, g2).start()
        return c

    lax.fori_loop(1, GRP, send_rows, 0)

    ebuf[g] = rows_v[g]

    most = jnp.zeros((ALL, 1), F32)
    for k in range(DP):
        owner = owner_of(columns[k])
        before = is_first & (line_owner == owner) & (line_of < first_column[k])
        slot = jnp.sum(jnp.where(before, 1.0, 0.0), axis=1, keepdims=True)
        most = jnp.maximum(most, slot)
        source = owner - (a * GRP).astype(F32)
        ours = (source >= 0.0) & (source < float(GRP)) & (slot < float(SLOTS))
        want = jnp.where(ours, source * float(SLOTS) + slot, -1.0)
        place = lax.broadcasted_iota(jnp.int32, (ALL, GRP * SLOTS), 1).astype(F32)
        chosen_v[k] = jnp.where(place == want, 1.0, 0.0).astype(BF)
    most_ref[...] = jnp.broadcast_to(jnp.max(most, axis=0, keepdims=True), (8, ALL))

    wait_bytes(ebuf.at[pl.ds(0, GRP - 1)], e_recv)
    table = ebuf[...].reshape(GRP * SLOTS, D)

    def picked(a2):
        return jnp.dot(chosen_v[a2], table, preferred_element_type=F32)

    for j in range(1, DP):
        a2 = (a + j) % DP
        tbuf[j] = picked(a2).astype(BF)
        remote(tbuf.at[j], dbuf.at[j], d_send, d_recv, a2, g).start()
    mine = picked(a) + extra_ref[...]
    wait_bytes(dbuf.at[pl.ds(1, DP - 1)], d_recv)
    for j in range(1, DP):
        mine = mine + dbuf[j].astype(F32)
    stream[...] = mine

    row32 = lax.broadcasted_iota(jnp.int32, (TOKENS, ALL), 0)
    lane32 = lax.broadcasted_iota(jnp.int32, (TOKENS, ALL), 1)
    own_token = lane32 == row32 + z * TOKENS

    def split(value):
        high = value.astype(BF).astype(F32)
        return jnp.concatenate([high, value - high], axis=0).astype(BF)

    for l in range(DECODER_LAYERS):
        s = stream[...]
        square = s * s
        high = square.astype(BF)
        low = (square - high.astype(F32)).astype(BF)
        ones = jnp.ones((8, D), BF)
        contract = (((1,), (1,)), ((), ()))
        sums = lax.dot_general(ones, high, contract, preferred_element_type=F32)
        sums = sums + lax.dot_general(ones, low, contract, preferred_element_type=F32)
        p1s[l, 0:ALL, :] = (s * gain_ref[l]).astype(BF)
        p1s[l, ALL : ALL + 16, :] = split(sums)

        def send_stream(j, c):
            remote(
                p1s.at[l], p1r.at[l, t], p1_send.at[l], p1_recv.at[l], a, z * SLICES + slice_at(j)
            ).start()
            return c

        lax.fori_loop(1, SLICES, send_stream, 0)
        p1r[l, t] = p1s[l]
        forward_weights(l, 0)
        wait_bytes(p1r.at[l, pl.ds(0, SLICES - 1)], p1_recv.at[l])
        await_weights(l, 0)

        left = jnp.concatenate([p1r[l, j, 0:ALL, :] for j in range(SLICES)], axis=1)
        sums = jnp.zeros((8, ALL), F32)
        for j in range(SLICES):
            tile = p1r[l, j, ALL : ALL + 16, :].astype(F32)
            sums = sums + tile[0:8] + tile[8:16]
        projected = jnp.dot(
            left, wqx[l].reshape(SLICES * D, QKV), preferred_element_type=F32
        ).astype(BF)
        sums = split(sums)
        for r in range(PLANES):
            for c in range(QKV // D):
                p2s[l, r, c * TOKENS : (c + 1) * TOKENS, :] = projected[
                    r * TOKENS : (r + 1) * TOKENS, c * D : (c + 1) * D
                ]
            p2s[l, r, 192:208, :] = sums
        for j in range(1, PLANES):
            z2 = (z + j) % PLANES
            remote(
                p2s.at[l, z2], p2r.at[l, j], p2_send.at[l], p2_recv.at[l], a, z2 * SLICES + t
            ).start()
        forward_weights(l, 1)
        wait_bytes(p2r.at[l, pl.ds(1, PLANES - 1)], p2_recv.at[l])
        if l + 1 < DECODER_LAYERS:
            send_weights(l + 1, 0)
        total = p2s[l, z].astype(F32)
        for j in range(1, PLANES):
            total = total + p2r[l, j].astype(F32)

        line = total[192:193] + total[200:201]
        column = jnp.sum(
            jnp.where(own_token, jnp.broadcast_to(line, (TOKENS, ALL)), 0.0), axis=1, keepdims=True
        )
        factor = lax.rsqrt(column * (1.0 / MODEL_WIDTH) + EPSILON)
        cosine, sine = cos_ref[...], sin_ref[...]

        def rotated(block):
            return block * cosine + pltpu.roll(block, 64, 1) * sine

        for h in range(4):
            qs[h * TOKENS : (h + 1) * TOKENS, :] = rotated(
                total[h * TOKENS : (h + 1) * TOKENS] * factor
            )
        kvs[0, 96:128, :] = rotated(total[128:160] * factor)
        kvs[1, 96:128, :] = total[160:192] * factor
        pltpu.make_async_copy(cache_ref.at[l], cache_v.at[l], cache_sem.at[l]).wait()
        fresh_row = lax.broadcasted_iota(jnp.int32, (16, D), 0) >= 12
        place = lax.broadcasted_iota(jnp.int32, (16, CACHE), 1)
        step = lax.broadcasted_iota(jnp.int32, (16, CACHE), 0) % DECODE_STEPS
        fresh_live = (place >= FRESH_AT) & (place - FRESH_AT <= step)
        for b in range(REPLICA_ROWS):
            for k in range(2):
                old = cache_v[l, b, CACHE - 16 : CACHE, k * D : (k + 1) * D].astype(F32)
                new = kvs[k, pl.ds(b, 16, stride=8), :]
                cache_v[l, b, CACHE - 16 : CACHE, k * D : (k + 1) * D] = jnp.where(
                    fresh_row, new, old
                ).astype(BF)
        for b in range(REPLICA_ROWS):
            query = qs[pl.ds(b, 16, stride=8), :].astype(BF)
            scores = lax.dot_general(
                query, cache_v[l, b, :, 0:D], contract, preferred_element_type=F32
            ) * (HEAD_SIZE**-0.5)
            live = (place < len_ref[b]) | fresh_live
            scores = jnp.where(live, scores, -1e30)
            top = jnp.max(scores, axis=1, keepdims=True)
            power = jnp.exp(scores - top)
            whole = jnp.sum(power, axis=1, keepdims=True)
            value = jnp.dot(power.astype(BF), cache_v[l, b, :, D : 2 * D], preferred_element_type=F32)
            atts[pl.ds(b, 16, stride=8), :] = value / whole

        p3s[l] = atts[...].astype(BF)
        for j in range(1, PLANES):
            z2 = (z + j) % PLANES
            remote(
                p3s.at[l], p3r.at[l, z], p3_send.at[l], p3_recv.at[l], a, z2 * SLICES + t
            ).start()
        p3r[l, z] = p3s[l]
        await_weights(l, 1)
        wait_bytes(p3r.at[l, pl.ds(0, PLANES - 1)], p3_recv.at[l])
        if l + 1 < DECODER_LAYERS:
            send_weights(l + 1, 1)
        left = jnp.concatenate(
            [
                jnp.concatenate(
                    [p3r[l, r, h * TOKENS : (h + 1) * TOKENS, :] for r in range(PLANES)], axis=0
                )
                for h in range(4)
            ],
            axis=1,
        )

        def partial(t2):
            return lax.dot_general(left, wox[l, t2], contract, preferred_element_type=F32)

        for j in range(1, SLICES):
            t2 = slice_at(j)
            p4s[l, j] = partial(t2).astype(BF)
            remote(
                p4s.at[l, j], p4r.at[l, j], p4_send.at[l], p4_recv.at[l], a, z * SLICES + t2
            ).start()
        s = stream[...] + partial(t)
        wait_bytes(p4r.at[l, pl.ds(1, SLICES - 1)], p4_recv.at[l])
        for j in range(1, SLICES):
            s = s + p4r[l, j].astype(F32)
        stream[...] = s

    last[...] = stream[...].astype(BF)
    home = g // 4
    for j in range(PLANES):
        r = (z + j) % PLANES
        g2 = r * SLICES + home
        tokens = last.at[pl.ds(pl.multiple_of(r * TOKENS, TOKENS), TOKENS), :]

        @pl.when(g2 != g)
        def _():
            remote(tokens, final.at[g % 4], o_send, o_recv, a, g2).start()

        @pl.when(g2 == g)
        def _():
            pltpu.make_async_copy(tokens, final.at[g % 4], o_recv).start()

    wait_bytes(final, o_recv)
    for k in range(4):
        out_ref[:, k * D : (k + 1) * D] = final[k]

    wait_bytes(land.at[pl.ds(0, DP - 1)], i_send)
    wait_bytes(ebuf.at[pl.ds(0, GRP - 1)], e_send)
    wait_bytes(dbuf.at[pl.ds(1, DP - 1)], d_send)
    for l in range(DECODER_LAYERS):
        for kind in range(2):
            buf = (wqx, wox)[kind]
            wait_bytes(buf.at[l, pl.ds(0, SLICES - 1), half, :], w_send.at[l, kind])
            wait_bytes(buf.at[l, :, half, :], f_send.at[l, kind])
        wait_bytes(p1r.at[l, pl.ds(0, SLICES - 1)], p1_send.at[l])
        wait_bytes(p2r.at[l, pl.ds(1, PLANES - 1)], p2_send.at[l])
        wait_bytes(p3r.at[l, pl.ds(0, PLANES - 1)], p3_send.at[l])
        wait_bytes(p4r.at[l, pl.ds(1, SLICES - 1)], p4_send.at[l])

    @pl.when(home == t)
    def _():
        wait_bytes(final.at[pl.ds(0, PLANES - 1)], o_send)

    @pl.when(home != t)
    def _():
        wait_bytes(final, o_send)


def decode(ids, extra, gain, cosine, sine, lengths, wq, wo, cache, embed):
    vmem = pl.BlockSpec(memory_space=pltpu.VMEM)
    hbm = pl.BlockSpec(memory_space=pltpu.HBM)
    layers = DECODER_LAYERS
    dma = pltpu.SemaphoreType.DMA
    return pl.pallas_call(
        main_kernel,
        out_shape=(
            jax.ShapeDtypeStruct((TOKENS, 512), BF),
            jax.ShapeDtypeStruct((DP, 8, ALL), jnp.int32),
            jax.ShapeDtypeStruct((8, ALL), F32),
        ),
        in_specs=[
            vmem,
            vmem,
            vmem,
            vmem,
            vmem,
            pl.BlockSpec(memory_space=pltpu.SMEM),
            hbm,
            hbm,
            hbm,
            hbm,
        ],
        out_specs=(vmem, vmem, vmem),
        scratch_shapes=[
            pltpu.VMEM((layers, REPLICA_ROWS, CACHE, 2 * D), BF),
            pltpu.VMEM((SHARD, MODEL_WIDTH), BF),
            pltpu.VMEM((DP, 8, ALL), jnp.int32),
            pltpu.VMEM((16, MODEL_WIDTH), BF),
            pltpu.VMEM((GRP, SLOTS, D), BF),
            pltpu.VMEM((DP, ALL, GRP * SLOTS), BF),
            pltpu.VMEM((layers, SLICES, D, QKV), BF),
            pltpu.VMEM((layers, SLICES, D, 512), BF),
            pltpu.VMEM((GRP, SLOTS, D), BF),
            pltpu.VMEM((DP, ALL, D), BF),
            pltpu.VMEM((DP, ALL, D), BF),
            pltpu.VMEM((ALL, D), F32),
            pltpu.VMEM((layers, ALL + 16, D), BF),
            pltpu.VMEM((layers, SLICES, ALL + 16, D), BF),
            pltpu.VMEM((layers, PLANES, 208, D), BF),
            pltpu.VMEM((layers, PLANES, 208, D), BF),
            pltpu.VMEM((4 * TOKENS, D), F32),
            pltpu.VMEM((2, 16 * REPLICA_ROWS, D), F32),
            pltpu.VMEM((4 * TOKENS, D), F32),
            pltpu.VMEM((layers, 4 * TOKENS, D), BF),
            pltpu.VMEM((layers, PLANES, 4 * TOKENS, D), BF),
            pltpu.VMEM((layers, SLICES, ALL, D), BF),
            pltpu.VMEM((layers, SLICES, ALL, D), BF),
            pltpu.VMEM((ALL, D), BF),
            pltpu.VMEM((4, TOKENS, D), BF),
            dma((layers,)),
            dma((layers, 2)),
            dma((layers, 2)),
            dma((layers, 2)),
            dma((layers, 2)),
            dma,
            dma,
            dma,
            dma,
            dma((layers,)),
            dma((layers,)),
            dma((layers,)),
            dma((layers,)),
            dma((layers,)),
            dma((layers,)),
            dma((layers,)),
            dma((layers,)),
            dma,
            dma,
            dma,
            dma,
            dma,
        ],
        compiler_params=pltpu.CompilerParams(
            collective_id=1, has_side_effects=True, vmem_limit_bytes=48 * 1024 * 1024
        ),
        name="decode",
    )(ids, extra, gain, cosine, sine, lengths, wq, wo, cache, embed)


def body(
    token_ids,
    start_pos,
    cache_len,
    embed_table,
    norm_gain,
    query_key_value_weight,
    output_weight,
    key_value_cache,
):
    a, g = lax.axis_index("dp"), lax.axis_index("grp")
    z = g // SLICES
    me = a * GRP + g
    shard_rows = embed_table.shape[0]
    number = DP * ALL

    lengths = lax.dynamic_index_in_dim(cache_len[0], z, 0, keepdims=False)
    starts = lax.dynamic_index_in_dim(start_pos[0], z, 0, keepdims=False)
    position = (starts[None, :] + jnp.arange(DECODE_STEPS, dtype=jnp.int32)[:, None]).reshape(TOKENS)
    exponent = jnp.arange(HEAD_SIZE // 2, dtype=F32) * (2.0 / HEAD_SIZE)
    frequency = jnp.power(F32(ROPE_BASE), -exponent)
    angles = position.astype(F32)[:, None] * frequency
    cosine, sine = jnp.cos(angles), jnp.sin(angles)
    cosine = jnp.concatenate([cosine, cosine], axis=1)
    sine = jnp.concatenate([-sine, sine], axis=1)
    gain = lax.dynamic_slice_in_dim(norm_gain, g * D, D, 1).reshape(DECODER_LAYERS, 1, D)

    def run(extra):
        return decode(
            ids,
            extra,
            gain,
            cosine,
            sine,
            lengths,
            query_key_value_weight,
            output_weight,
            key_value_cache.reshape(DECODER_LAYERS, REPLICA_ROWS, CACHE, 2 * D),
            embed_table,
        )

    ids = jnp.broadcast_to(token_ids[0].transpose(0, 2, 1).reshape(1, ALL), (8, ALL))
    out, everyone, most = run(jnp.zeros((ALL, D), F32))

    def again(_):
        flat = everyone[:, 0, :].reshape(DP * ALL)
        owner = flat // shard_rows
        order = jnp.arange(DP * ALL, dtype=jnp.int32)
        first = jnp.min(jnp.where(flat[:, None] == flat[None, :], order[None, :], DP * ALL), axis=1)
        before = (
            (first == order)[None, :]
            & (owner[:, None] == owner[None, :])
            & (order[None, :] < first[:, None])
        )
        slot = jnp.sum(before.astype(jnp.int32), axis=1)
        late = (owner == me) & (slot >= SLOTS)
        more = jnp.take(embed_table, jnp.where(late, flat - me * shard_rows, 0), axis=0, mode="clip")
        more = jnp.where(late[:, None], more, jnp.zeros_like(more)).reshape(DP, ALL, GRP, D)
        more = more.transpose(0, 2, 1, 3).reshape(DP * GRP, ALL, D)
        more = lax.all_to_all(more, ("dp", "grp"), split_axis=0, concat_axis=0, tiled=True)
        return run(jnp.sum(more.astype(F32), axis=0))[0]

    out = lax.cond(most[0, 0] >= SLOTS, again, lambda _: out, jnp.int32(0))
    return out.reshape(DECODE_STEPS, REPLICA_ROWS, 512).transpose(1, 0, 2)[:, None]


def solution(mesh):
    return jax.shard_map(
        body,
        mesh=mesh,
        in_specs=(
            P("dp", None, None, None),
            P("dp", None, None),
            P("dp", None, None),
            P(("dp", "grp"), None),
            P(),
            P(None, "grp", None),
            P(None, "grp", None),
            P(None, "dp", "grp", None, None),
        ),
        out_specs=P("dp", "grp", None, None),
        check_vma=False,
    )
```

```python
import jax
import jax.numpy as jnp
from jax import lax
from jax.experimental import pallas as pl
from jax.experimental.pallas import tpu as pltpu
from jax.sharding import PartitionSpec as P

MODEL_WIDTH = 4096
QUERY_HEADS = 32
KEY_VALUE_HEADS = 8
HEAD_SIZE = 128
DECODER_LAYERS = 2
DECODE_STEPS = 4
REPLICA_ROWS = 8
ROPE_BASE = 500000.0
EPSILON = 1e-05

MESH = pl.DeviceIdType.MESH
SLOTS = 16
DP = 4
PLANES = 4
SLICES = 8
GRP = PLANES * SLICES
TOKENS = REPLICA_ROWS * DECODE_STEPS
ALL = PLANES * TOKENS
D = 128
QKV = 768
CACHE = 1024
SHARD = 1002
SHARD_WHOLE = 992
FRESH_AT = CACHE - DECODE_STEPS
BF = jnp.bfloat16
F32 = jnp.float32


def main_kernel(
    ids_ref,
    extra_ref,
    gain_ref,
    cos_ref,
    sin_ref,
    len_ref,
    wq_ref,
    wo_ref,
    cache_ref,
    embed_ref,
    out_ref,
    all_ref,
    most_ref,
    cache_v,
    shard_v,
    land,
    tail_v,
    rows_v,
    chosen_v,
    wqx,
    wox,
    ebuf,
    tbuf,
    dbuf,
    stream,
    p1s,
    p1r,
    p2s,
    p2r,
    qs,
    kvs,
    atts,
    p3s,
    p3r,
    p4s,
    p4r,
    last,
    final,
    cache_sem,
    w_send,
    w_recv,
    f_send,
    f_recv,
    e_send,
    e_recv,
    d_send,
    d_recv,
    p1_send,
    p1_recv,
    p2_send,
    p2_recv,
    p3_send,
    p3_recv,
    p4_send,
    p4_recv,
    o_send,
    o_recv,
    i_send,
    i_recv,
    s_sem,
):
    a, g = lax.axis_index("dp"), lax.axis_index("grp")
    core = a % 2
    sibling = a + 1 - 2 * core
    z, t = g // SLICES, g % SLICES
    y, x = t // 4, t % 4

    def remote(src, dst, send_sem, recv_sem, a2, g2):
        return pltpu.make_async_remote_copy(
            src_ref=src,
            dst_ref=dst,
            send_sem=send_sem,
            recv_sem=recv_sem,
            device_id=(a2, g2),
            device_id_type=MESH,
        )

    def wait_bytes(ref, sem):
        pltpu.make_async_copy(ref, ref, sem).wait()

    def slice_at(j):
        return ((y + j // 4) % 2) * 4 + (x + j % 4) % 4

    shard_copy = pltpu.make_async_copy(embed_ref, shard_v, s_sem)
    shard_copy.start()
    for l in range(DECODER_LAYERS):
        pltpu.make_async_copy(cache_ref.at[l], cache_v.at[l], cache_sem.at[l]).start()

    barrier = pltpu.get_barrier_semaphore()

    def greet(j, c):
        pl.semaphore_signal(barrier, inc=1, device_id=(a, (g + j) % GRP), device_id_type=MESH)
        return c

    lax.fori_loop(1, GRP, greet, 0)
    for j in range(1, DP):
        pl.semaphore_signal(barrier, inc=1, device_id=((a + j) % DP, g), device_id_type=MESH)

    def greet_across(k, c):
        g2 = z * SLICES + (1 - y) * 4 + k
        pl.semaphore_signal(barrier, inc=1, device_id=((a + 2) % DP, g2), device_id_type=MESH)
        return c

    lax.fori_loop(0, 4, greet_across, 0)
    pl.semaphore_wait(barrier, GRP - 1 + DP - 1 + 4)

    land[a] = ids_ref[...]
    for j in range(1, DP):
        remote(ids_ref, land.at[a], i_send, i_recv, (a + j) % DP, g).start()

    half = pl.ds(pl.multiple_of(core * 64, 64), 64)
    halves = [pl.ds(pl.multiple_of(core * 64 + k * 32, 32), 32) for k in range(2)]
    across = (a + 2) % DP

    def qkv_pieces(l, t2, half):
        return (
            (
                wq_ref.at[l, half, pl.ds(pl.multiple_of(t2 * 512, 512), 512)],
                wqx.at[l, t, half, pl.ds(0, 512)],
            ),
            (
                wq_ref.at[l, half, pl.ds(pl.multiple_of(4096 + t2 * 128, 128), 128)],
                wqx.at[l, t, half, pl.ds(512, 128)],
            ),
            (
                wq_ref.at[l, half, pl.ds(pl.multiple_of(5120 + t2 * 128, 128), 128)],
                wqx.at[l, t, half, pl.ds(640, 128)],
            ),
        )

    def out_pieces(l, t2, half):
        return (
            (
                wo_ref.at[l, half, pl.ds(pl.multiple_of(t2 * 512, 512), 512)],
                wox.at[l, t, half, :],
            ),
        )

    def send_weights(l, kind):
        pieces = (qkv_pieces, out_pieces)[kind]

        def send(j, rows, a2):
            t2 = slice_at(j)
            for src, dst in pieces(l, t2, rows):
                remote(src, dst, w_send.at[l, kind], w_recv.at[l, kind], a2, z * SLICES + t2).start()

        def one(j, c):
            send(j, half, a)
            return c

        def both(j, c):
            send(j, halves[0], a)
            send(j, halves[1], across)
            return c

        lax.fori_loop(4, SLICES, both, 0)
        lax.fori_loop(1, 4, one, 0)
        for src, dst in pieces(l, t, half):
            pltpu.make_async_copy(src, dst, w_recv.at[l, kind]).start()

    def forward_weights(l, kind):
        buf = (wqx, wox)[kind]
        wait_bytes(buf.at[l, :, half, :], w_recv.at[l, kind])
        remote(
            buf.at[l, :, half, :],
            buf.at[l, :, half, :],
            f_send.at[l, kind],
            f_recv.at[l, kind],
            sibling,
            g,
        ).start()

    def await_weights(l, kind):
        buf = (wqx, wox)[kind]
        wait_bytes(buf.at[l, :, half, :], f_recv.at[l, kind])

    send_weights(0, 0)
    kvs[...] = jnp.zeros_like(kvs)
    wait_bytes(land.at[pl.ds(0, DP - 1)], i_recv)

    number = DP * ALL
    all_ref[...] = land[...]
    along = jnp.concatenate([land[k] for k in range(DP)], axis=1).astype(F32)
    line_of = lax.broadcasted_iota(jnp.int32, (1, number), 1).astype(F32)
    line_id = along[0:1]
    columns = []
    for k in range(DP):
        square = jnp.concatenate([along[:, k * ALL : (k + 1) * ALL]] * 16, axis=0)
        columns.append(jnp.transpose(square)[:, 0:1])

    def owner_of(ids):
        return jnp.floor((ids + 0.5) * (1.0 / SHARD))

    first_line = jnp.full((1, number), float(number), F32)
    first_column = []
    for k in range(DP):
        same = columns[k] == line_id
        up = lax.broadcasted_iota(jnp.int32, (ALL, number), 0).astype(F32) + float(k * ALL)
        first_line = jnp.minimum(
            first_line, jnp.min(jnp.where(same, up, float(number)), axis=0, keepdims=True)
        )
        first_column.append(jnp.min(jnp.where(same, line_of, float(number)), axis=1, keepdims=True))
    is_first = first_line == line_of
    line_owner = owner_of(line_id)
    me = (a * GRP + g).astype(F32)

    held = jnp.where(is_first & (line_owner == me), 1.0, 0.0)
    earlier = lax.broadcasted_iota(jnp.int32, (number, number), 0) < lax.broadcasted_iota(
        jnp.int32, (number, number), 1
    )
    earlier = jnp.where(earlier, 1.0, 0.0).astype(BF)
    rank = jnp.dot(
        jnp.broadcast_to(held, (8, number)).astype(BF), earlier, preferred_element_type=F32
    )[0:1]
    slot_no = lax.broadcasted_iota(jnp.int32, (SLOTS, number), 0).astype(F32)
    local = jnp.sum(
        jnp.where((held > 0.0) & (rank == slot_no), line_id - me * float(SHARD), 0.0),
        axis=1,
        keepdims=True,
    )
    entry = lax.broadcasted_iota(jnp.int32, (SLOTS, SHARD_WHOLE), 1).astype(F32)
    take = jnp.where(entry == local, 1.0, 0.0).astype(BF)
    tail = lax.broadcasted_iota(jnp.int32, (SLOTS, 16), 1).astype(F32) + float(SHARD_WHOLE)
    take_tail = jnp.where(tail == local, 1.0, 0.0).astype(BF)
    shard_copy.wait()
    tail_v[...] = jnp.zeros_like(tail_v)
    tail_v[0 : SHARD - SHARD_WHOLE, :] = shard_v[SHARD_WHOLE:SHARD, :]
    rows = jnp.dot(take, shard_v[0:SHARD_WHOLE, :], preferred_element_type=F32)
    rows = rows + jnp.dot(take_tail, tail_v[...], preferred_element_type=F32)
    rows = rows.astype(BF)
    for k in range(GRP):
        rows_v[k] = rows[:, k * D : (k + 1) * D]

    def send_rows(j, c):
        g2 = ((z + j // SLICES) % PLANES) * SLICES + slice_at(j % SLICES)
        remote(rows_v.at[g2], ebuf.at[g], e_send, e_recv, a, g2).start()
        return c

    lax.fori_loop(1, GRP, send_rows, 0)
    send_weights(0, 1)

    ebuf[g] = rows_v[g]

    most = jnp.zeros((ALL, 1), F32)
    for k in range(DP):
        owner = owner_of(columns[k])
        before = is_first & (line_owner == owner) & (line_of < first_column[k])
        slot = jnp.sum(jnp.where(before, 1.0, 0.0), axis=1, keepdims=True)
        most = jnp.maximum(most, slot)
        source = owner - (a * GRP).astype(F32)
        ours = (source >= 0.0) & (source < float(GRP)) & (slot < float(SLOTS))
        want = jnp.where(ours, source * float(SLOTS) + slot, -1.0)
        place = lax.broadcasted_iota(jnp.int32, (ALL, GRP * SLOTS), 1).astype(F32)
        chosen_v[k] = jnp.where(place == want, 1.0, 0.0).astype(BF)
    most_ref[...] = jnp.broadcast_to(jnp.max(most, axis=0, keepdims=True), (8, ALL))

    wait_bytes(ebuf.at[pl.ds(0, GRP - 1)], e_recv)
    table = ebuf[...].reshape(GRP * SLOTS, D)

    def picked(a2):
        return jnp.dot(chosen_v[a2], table, preferred_element_type=F32)

    for j in range(1, DP):
        a2 = (a + j) % DP
        tbuf[j] = picked(a2).astype(BF)
        remote(tbuf.at[j], dbuf.at[j], d_send, d_recv, a2, g).start()
    mine = picked(a) + extra_ref[...]
    wait_bytes(dbuf.at[pl.ds(1, DP - 1)], d_recv)
    for j in range(1, DP):
        mine = mine + dbuf[j].astype(F32)
    stream[...] = mine

    row32 = lax.broadcasted_iota(jnp.int32, (TOKENS, ALL), 0)
    lane32 = lax.broadcasted_iota(jnp.int32, (TOKENS, ALL), 1)
    own_token = lane32 == row32 + z * TOKENS

    def split(value):
        high = value.astype(BF).astype(F32)
        return jnp.concatenate([high, value - high], axis=0).astype(BF)

    for l in range(DECODER_LAYERS):
        s = stream[...]
        square = s * s
        high = square.astype(BF)
        low = (square - high.astype(F32)).astype(BF)
        ones = jnp.ones((8, D), BF)
        contract = (((1,), (1,)), ((), ()))
        sums = lax.dot_general(ones, high, contract, preferred_element_type=F32)
        sums = sums + lax.dot_general(ones, low, contract, preferred_element_type=F32)
        p1s[l, 0:ALL, :] = (s * gain_ref[l]).astype(BF)
        p1s[l, ALL : ALL + 16, :] = split(sums)

        def send_stream(j, c):
            remote(
                p1s.at[l], p1r.at[l, t], p1_send.at[l], p1_recv.at[l], a, z * SLICES + slice_at(j)
            ).start()
            return c

        lax.fori_loop(1, SLICES, send_stream, 0)
        p1r[l, t] = p1s[l]
        forward_weights(l, 0)
        wait_bytes(p1r.at[l, pl.ds(0, SLICES - 1)], p1_recv.at[l])
        await_weights(l, 0)
        if l + 1 < DECODER_LAYERS:
            send_weights(l + 1, 0)
        if l + 1 < DECODER_LAYERS:
            send_weights(l + 1, 1)

        left = jnp.concatenate([p1r[l, j, 0:ALL, :] for j in range(SLICES)], axis=1)
        sums = jnp.zeros((8, ALL), F32)
        for j in range(SLICES):
            tile = p1r[l, j, ALL : ALL + 16, :].astype(F32)
            sums = sums + tile[0:8] + tile[8:16]
        projected = jnp.dot(
            left, wqx[l].reshape(SLICES * D, QKV), preferred_element_type=F32
        ).astype(BF)
        sums = split(sums)
        for r in range(PLANES):
            for c in range(QKV // D):
                p2s[l, r, c * TOKENS : (c + 1) * TOKENS, :] = projected[
                    r * TOKENS : (r + 1) * TOKENS, c * D : (c + 1) * D
                ]
            p2s[l, r, 192:208, :] = sums
        for j in range(1, PLANES):
            z2 = (z + j) % PLANES
            remote(
                p2s.at[l, z2], p2r.at[l, j], p2_send.at[l], p2_recv.at[l], a, z2 * SLICES + t
            ).start()
        forward_weights(l, 1)
        wait_bytes(p2r.at[l, pl.ds(1, PLANES - 1)], p2_recv.at[l])
        total = p2s[l, z].astype(F32)
        for j in range(1, PLANES):
            total = total + p2r[l, j].astype(F32)

        line = total[192:193] + total[200:201]
        column = jnp.sum(
            jnp.where(own_token, jnp.broadcast_to(line, (TOKENS, ALL)), 0.0), axis=1, keepdims=True
        )
        factor = lax.rsqrt(column * (1.0 / MODEL_WIDTH) + EPSILON)
        cosine, sine = cos_ref[...], sin_ref[...]

        def rotated(block):
            return block * cosine + pltpu.roll(block, 64, 1) * sine

        for h in range(4):
            qs[h * TOKENS : (h + 1) * TOKENS, :] = rotated(
                total[h * TOKENS : (h + 1) * TOKENS] * factor
            )
        kvs[0, 96:128, :] = rotated(total[128:160] * factor)
        kvs[1, 96:128, :] = total[160:192] * factor
        pltpu.make_async_copy(cache_ref.at[l], cache_v.at[l], cache_sem.at[l]).wait()
        fresh_row = lax.broadcasted_iota(jnp.int32, (16, D), 0) >= 12
        place = lax.broadcasted_iota(jnp.int32, (16, CACHE), 1)
        step = lax.broadcasted_iota(jnp.int32, (16, CACHE), 0) % DECODE_STEPS
        fresh_live = (place >= FRESH_AT) & (place - FRESH_AT <= step)
        for b in range(REPLICA_ROWS):
            for k in range(2):
                old = cache_v[l, b, CACHE - 16 : CACHE, k * D : (k + 1) * D].astype(F32)
                new = kvs[k, pl.ds(b, 16, stride=8), :]
                cache_v[l, b, CACHE - 16 : CACHE, k * D : (k + 1) * D] = jnp.where(
                    fresh_row, new, old
                ).astype(BF)
        for b in range(REPLICA_ROWS):
            query = qs[pl.ds(b, 16, stride=8), :].astype(BF)
            scores = lax.dot_general(
                query, cache_v[l, b, :, 0:D], contract, preferred_element_type=F32
            ) * (HEAD_SIZE**-0.5)
            live = (place < len_ref[b]) | fresh_live
            scores = jnp.where(live, scores, -1e30)
            top = jnp.max(scores, axis=1, keepdims=True)
            power = jnp.exp(scores - top)
            whole = jnp.sum(power, axis=1, keepdims=True)
            value = jnp.dot(power.astype(BF), cache_v[l, b, :, D : 2 * D], preferred_element_type=F32)
            atts[pl.ds(b, 16, stride=8), :] = value / whole

        p3s[l] = atts[...].astype(BF)
        for j in range(1, PLANES):
            z2 = (z + j) % PLANES
            remote(
                p3s.at[l], p3r.at[l, z], p3_send.at[l], p3_recv.at[l], a, z2 * SLICES + t
            ).start()
        p3r[l, z] = p3s[l]
        await_weights(l, 1)
        wait_bytes(p3r.at[l, pl.ds(0, PLANES - 1)], p3_recv.at[l])
        left = jnp.concatenate(
            [
                jnp.concatenate(
                    [p3r[l, r, h * TOKENS : (h + 1) * TOKENS, :] for r in range(PLANES)], axis=0
                )
                for h in range(4)
            ],
            axis=1,
        )

        def partial(t2):
            return lax.dot_general(left, wox[l, t2], contract, preferred_element_type=F32)

        for j in range(1, SLICES):
            t2 = slice_at(j)
            p4s[l, j] = partial(t2).astype(BF)
            remote(
                p4s.at[l, j], p4r.at[l, j], p4_send.at[l], p4_recv.at[l], a, z * SLICES + t2
            ).start()
        s = stream[...] + partial(t)
        wait_bytes(p4r.at[l, pl.ds(1, SLICES - 1)], p4_recv.at[l])
        for j in range(1, SLICES):
            s = s + p4r[l, j].astype(F32)
        stream[...] = s

    last[...] = stream[...].astype(BF)
    home = g // 4
    for j in range(PLANES):
        r = (z + j) % PLANES
        g2 = r * SLICES + home
        tokens = last.at[pl.ds(pl.multiple_of(r * TOKENS, TOKENS), TOKENS), :]

        @pl.when(g2 != g)
        def _():
            remote(tokens, final.at[g % 4], o_send, o_recv, a, g2).start()

        @pl.when(g2 == g)
        def _():
            pltpu.make_async_copy(tokens, final.at[g % 4], o_recv).start()

    wait_bytes(final, o_recv)
    for k in range(4):
        out_ref[:, k * D : (k + 1) * D] = final[k]

    wait_bytes(land.at[pl.ds(0, DP - 1)], i_send)
    wait_bytes(ebuf.at[pl.ds(0, GRP - 1)], e_send)
    wait_bytes(dbuf.at[pl.ds(1, DP - 1)], d_send)
    for l in range(DECODER_LAYERS):
        for kind in range(2):
            buf = (wqx, wox)[kind]
            wait_bytes(buf.at[l, pl.ds(0, SLICES - 1), half, :], w_send.at[l, kind])
            wait_bytes(buf.at[l, :, half, :], f_send.at[l, kind])
        wait_bytes(p1r.at[l, pl.ds(0, SLICES - 1)], p1_send.at[l])
        wait_bytes(p2r.at[l, pl.ds(1, PLANES - 1)], p2_send.at[l])
        wait_bytes(p3r.at[l, pl.ds(0, PLANES - 1)], p3_send.at[l])
        wait_bytes(p4r.at[l, pl.ds(1, SLICES - 1)], p4_send.at[l])

    @pl.when(home == t)
    def _():
        wait_bytes(final.at[pl.ds(0, PLANES - 1)], o_send)

    @pl.when(home != t)
    def _():
        wait_bytes(final, o_send)


def decode(ids, extra, gain, cosine, sine, lengths, wq, wo, cache, embed):
    vmem = pl.BlockSpec(memory_space=pltpu.VMEM)
    hbm = pl.BlockSpec(memory_space=pltpu.HBM)
    layers = DECODER_LAYERS
    dma = pltpu.SemaphoreType.DMA
    return pl.pallas_call(
        main_kernel,
        out_shape=(
            jax.ShapeDtypeStruct((TOKENS, 512), BF),
            jax.ShapeDtypeStruct((DP, 8, ALL), jnp.int32),
            jax.ShapeDtypeStruct((8, ALL), F32),
        ),
        in_specs=[
            vmem,
            vmem,
            vmem,
            vmem,
            vmem,
            pl.BlockSpec(memory_space=pltpu.SMEM),
            hbm,
            hbm,
            hbm,
            hbm,
        ],
        out_specs=(vmem, vmem, vmem),
        scratch_shapes=[
            pltpu.VMEM((layers, REPLICA_ROWS, CACHE, 2 * D), BF),
            pltpu.VMEM((SHARD, MODEL_WIDTH), BF),
            pltpu.VMEM((DP, 8, ALL), jnp.int32),
            pltpu.VMEM((16, MODEL_WIDTH), BF),
            pltpu.VMEM((GRP, SLOTS, D), BF),
            pltpu.VMEM((DP, ALL, GRP * SLOTS), BF),
            pltpu.VMEM((layers, SLICES, D, QKV), BF),
            pltpu.VMEM((layers, SLICES, D, 512), BF),
            pltpu.VMEM((GRP, SLOTS, D), BF),
            pltpu.VMEM((DP, ALL, D), BF),
            pltpu.VMEM((DP, ALL, D), BF),
            pltpu.VMEM((ALL, D), F32),
            pltpu.VMEM((layers, ALL + 16, D), BF),
            pltpu.VMEM((layers, SLICES, ALL + 16, D), BF),
            pltpu.VMEM((layers, PLANES, 208, D), BF),
            pltpu.VMEM((layers, PLANES, 208, D), BF),
            pltpu.VMEM((4 * TOKENS, D), F32),
            pltpu.VMEM((2, 16 * REPLICA_ROWS, D), F32),
            pltpu.VMEM((4 * TOKENS, D), F32),
            pltpu.VMEM((layers, 4 * TOKENS, D), BF),
            pltpu.VMEM((layers, PLANES, 4 * TOKENS, D), BF),
            pltpu.VMEM((layers, SLICES, ALL, D), BF),
            pltpu.VMEM((layers, SLICES, ALL, D), BF),
            pltpu.VMEM((ALL, D), BF),
            pltpu.VMEM((4, TOKENS, D), BF),
            dma((layers,)),
            dma((layers, 2)),
            dma((layers, 2)),
            dma((layers, 2)),
            dma((layers, 2)),
            dma,
            dma,
            dma,
            dma,
            dma((layers,)),
            dma((layers,)),
            dma((layers,)),
            dma((layers,)),
            dma((layers,)),
            dma((layers,)),
            dma((layers,)),
            dma((layers,)),
            dma,
            dma,
            dma,
            dma,
            dma,
        ],
        compiler_params=pltpu.CompilerParams(
            collective_id=1, has_side_effects=True, vmem_limit_bytes=48 * 1024 * 1024
        ),
        name="decode",
    )(ids, extra, gain, cosine, sine, lengths, wq, wo, cache, embed)


def body(
    token_ids,
    start_pos,
    cache_len,
    embed_table,
    norm_gain,
    query_key_value_weight,
    output_weight,
    key_value_cache,
):
    a, g = lax.axis_index("dp"), lax.axis_index("grp")
    z = g // SLICES
    me = a * GRP + g
    shard_rows = embed_table.shape[0]
    number = DP * ALL

    lengths = lax.dynamic_index_in_dim(cache_len[0], z, 0, keepdims=False)
    starts = lax.dynamic_index_in_dim(start_pos[0], z, 0, keepdims=False)
    position = (starts[None, :] + jnp.arange(DECODE_STEPS, dtype=jnp.int32)[:, None]).reshape(TOKENS)
    exponent = jnp.arange(HEAD_SIZE // 2, dtype=F32) * (2.0 / HEAD_SIZE)
    frequency = jnp.power(F32(ROPE_BASE), -exponent)
    angles = position.astype(F32)[:, None] * frequency
    cosine, sine = jnp.cos(angles), jnp.sin(angles)
    cosine = jnp.concatenate([cosine, cosine], axis=1)
    sine = jnp.concatenate([-sine, sine], axis=1)
    gain = lax.dynamic_slice_in_dim(norm_gain, g * D, D, 1).reshape(DECODER_LAYERS, 1, D)

    def run(extra):
        return decode(
            ids,
            extra,
            gain,
            cosine,
            sine,
            lengths,
            query_key_value_weight,
            output_weight,
            key_value_cache.reshape(DECODER_LAYERS, REPLICA_ROWS, CACHE, 2 * D),
            embed_table,
        )

    ids = jnp.broadcast_to(token_ids[0].transpose(0, 2, 1).reshape(1, ALL), (8, ALL))
    out, everyone, most = run(jnp.zeros((ALL, D), F32))

    def again(_):
        flat = everyone[:, 0, :].reshape(DP * ALL)
        owner = flat // shard_rows
        order = jnp.arange(DP * ALL, dtype=jnp.int32)
        first = jnp.min(jnp.where(flat[:, None] == flat[None, :], order[None, :], DP * ALL), axis=1)
        before = (
            (first == order)[None, :]
            & (owner[:, None] == owner[None, :])
            & (order[None, :] < first[:, None])
        )
        slot = jnp.sum(before.astype(jnp.int32), axis=1)
        late = (owner == me) & (slot >= SLOTS)
        more = jnp.take(embed_table, jnp.where(late, flat - me * shard_rows, 0), axis=0, mode="clip")
        more = jnp.where(late[:, None], more, jnp.zeros_like(more)).reshape(DP, ALL, GRP, D)
        more = more.transpose(0, 2, 1, 3).reshape(DP * GRP, ALL, D)
        more = lax.all_to_all(more, ("dp", "grp"), split_axis=0, concat_axis=0, tiled=True)
        return run(jnp.sum(more.astype(F32), axis=0))[0]

    out = lax.cond(most[0, 0] >= SLOTS, again, lambda _: out, jnp.int32(0))
    return out.reshape(DECODE_STEPS, REPLICA_ROWS, 512).transpose(1, 0, 2)[:, None]


def solution(mesh):
    return jax.shard_map(
        body,
        mesh=mesh,
        in_specs=(
            P("dp", None, None, None),
            P("dp", None, None),
            P("dp", None, None),
            P(("dp", "grp"), None),
            P(),
            P(None, "grp", None),
            P(None, "grp", None),
            P(None, "dp", "grp", None, None),
        ),
        out_specs=P("dp", "grp", None, None),
        check_vma=False,
    )
```

```python
import jax
import jax.numpy as jnp
from jax import lax
from jax.experimental import pallas as pl
from jax.experimental.pallas import tpu as pltpu
from jax.sharding import PartitionSpec as P

MODEL_WIDTH = 4096
QUERY_HEADS = 32
KEY_VALUE_HEADS = 8
HEAD_SIZE = 128
DECODER_LAYERS = 2
DECODE_STEPS = 4
REPLICA_ROWS = 8
ROPE_BASE = 500000.0
EPSILON = 1e-05

MESH = pl.DeviceIdType.MESH
SLOTS = 16
DP = 4
PLANES = 4
SLICES = 8
GRP = PLANES * SLICES
FAR_FIRST = (6, 5, 7, 2, 4, 1, 3)
TOKENS = REPLICA_ROWS * DECODE_STEPS
ALL = PLANES * TOKENS
D = 128
QKV = 768
CACHE = 1024
SHARD = 1002
SHARD_WHOLE = 992
FRESH_AT = CACHE - DECODE_STEPS
BF = jnp.bfloat16
F32 = jnp.float32


def main_kernel(
    ids_ref,
    extra_ref,
    gain_ref,
    cos_ref,
    sin_ref,
    len_ref,
    wq_ref,
    wo_ref,
    cache_ref,
    embed_ref,
    out_ref,
    all_ref,
    most_ref,
    cache_v,
    shard_v,
    land,
    tail_v,
    rows_v,
    chosen_v,
    wqx,
    wox,
    ebuf,
    tbuf,
    dbuf,
    stream,
    p1s,
    p1r,
    p2s,
    p2r,
    qs,
    kvs,
    atts,
    p3s,
    p3r,
    p4s,
    p4r,
    last,
    final,
    cache_sem,
    w_send,
    w_recv,
    f_send,
    f_recv,
    e_send,
    e_recv,
    d_send,
    d_recv,
    p1_send,
    p1_recv,
    p2_send,
    p2_recv,
    p3_send,
    p3_recv,
    p4_send,
    p4_recv,
    o_send,
    o_recv,
    i_send,
    i_recv,
    s_sem,
):
    a, g = lax.axis_index("dp"), lax.axis_index("grp")
    core = a % 2
    sibling = a + 1 - 2 * core
    z, t = g // SLICES, g % SLICES
    y, x = t // 4, t % 4

    def remote(src, dst, send_sem, recv_sem, a2, g2):
        return pltpu.make_async_remote_copy(
            src_ref=src,
            dst_ref=dst,
            send_sem=send_sem,
            recv_sem=recv_sem,
            device_id=(a2, g2),
            device_id_type=MESH,
        )

    def wait_bytes(ref, sem):
        pltpu.make_async_copy(ref, ref, sem).wait()

    def slice_at(j):
        return ((y + j // 4) % 2) * 4 + (x + j % 4) % 4

    shard_copy = pltpu.make_async_copy(embed_ref, shard_v, s_sem)
    shard_copy.start()
    for l in range(DECODER_LAYERS):
        pltpu.make_async_copy(cache_ref.at[l], cache_v.at[l], cache_sem.at[l]).start()

    barrier = pltpu.get_barrier_semaphore()

    def greet(j, c):
        pl.semaphore_signal(barrier, inc=1, device_id=(a, (g + j) % GRP), device_id_type=MESH)
        return c

    lax.fori_loop(1, GRP, greet, 0)
    for j in range(1, DP):
        pl.semaphore_signal(barrier, inc=1, device_id=((a + j) % DP, g), device_id_type=MESH)

    def greet_across(k, c):
        g2 = z * SLICES + (1 - y) * 4 + k
        pl.semaphore_signal(barrier, inc=1, device_id=((a + 2) % DP, g2), device_id_type=MESH)
        return c

    lax.fori_loop(0, 4, greet_across, 0)
    pl.semaphore_wait(barrier, GRP - 1 + DP - 1 + 4)

    land[a] = ids_ref[...]
    for j in range(1, DP):
        remote(ids_ref, land.at[a], i_send, i_recv, (a + j) % DP, g).start()

    half = pl.ds(pl.multiple_of(core * 64, 64), 64)
    halves = [pl.ds(pl.multiple_of(core * 64 + k * 32, 32), 32) for k in range(2)]
    across = (a + 2) % DP

    def qkv_pieces(l, t2, half):
        return (
            (
                wq_ref.at[l, half, pl.ds(pl.multiple_of(t2 * 512, 512), 512)],
                wqx.at[l, t, half, pl.ds(0, 512)],
            ),
            (
                wq_ref.at[l, half, pl.ds(pl.multiple_of(4096 + t2 * 128, 128), 128)],
                wqx.at[l, t, half, pl.ds(512, 128)],
            ),
            (
                wq_ref.at[l, half, pl.ds(pl.multiple_of(5120 + t2 * 128, 128), 128)],
                wqx.at[l, t, half, pl.ds(640, 128)],
            ),
        )

    def out_pieces(l, t2, half):
        return (
            (
                wo_ref.at[l, half, pl.ds(pl.multiple_of(t2 * 512, 512), 512)],
                wox.at[l, t, half, :],
            ),
        )

    def send_weights(l, kind):
        pieces = (qkv_pieces, out_pieces)[kind]

        def send(j, rows, a2):
            t2 = slice_at(j)
            for src, dst in pieces(l, t2, rows):
                remote(src, dst, w_send.at[l, kind], w_recv.at[l, kind], a2, z * SLICES + t2).start()

        def one(j, c):
            send(j, half, a)
            return c

        def both(j, c):
            send(j, halves[0], a)
            send(j, halves[1], across)
            return c

        lax.fori_loop(4, SLICES, both, 0)
        lax.fori_loop(1, 4, one, 0)
        for src, dst in pieces(l, t, half):
            pltpu.make_async_copy(src, dst, w_recv.at[l, kind]).start()

    def forward_weights(l, kind):
        buf = (wqx, wox)[kind]
        wait_bytes(buf.at[l, :, half, :], w_recv.at[l, kind])
        remote(
            buf.at[l, :, half, :],
            buf.at[l, :, half, :],
            f_send.at[l, kind],
            f_recv.at[l, kind],
            sibling,
            g,
        ).start()

    def await_weights(l, kind):
        buf = (wqx, wox)[kind]
        wait_bytes(buf.at[l, :, half, :], f_recv.at[l, kind])

    send_weights(0, 0)
    kvs[...] = jnp.zeros_like(kvs)
    wait_bytes(land.at[pl.ds(0, DP - 1)], i_recv)

    number = DP * ALL
    all_ref[...] = land[...]
    along = jnp.concatenate([land[k] for k in range(DP)], axis=1).astype(F32)
    line_of = lax.broadcasted_iota(jnp.int32, (1, number), 1).astype(F32)
    line_id = along[0:1]
    columns = []
    for k in range(DP):
        square = jnp.concatenate([along[:, k * ALL : (k + 1) * ALL]] * 16, axis=0)
        columns.append(jnp.transpose(square)[:, 0:1])

    def owner_of(ids):
        return jnp.floor((ids + 0.5) * (1.0 / SHARD))

    first_line = jnp.full((1, number), float(number), F32)
    first_column = []
    for k in range(DP):
        same = columns[k] == line_id
        up = lax.broadcasted_iota(jnp.int32, (ALL, number), 0).astype(F32) + float(k * ALL)
        first_line = jnp.minimum(
            first_line, jnp.min(jnp.where(same, up, float(number)), axis=0, keepdims=True)
        )
        first_column.append(jnp.min(jnp.where(same, line_of, float(number)), axis=1, keepdims=True))
    is_first = first_line == line_of
    line_owner = owner_of(line_id)
    me = (a * GRP + g).astype(F32)

    held = jnp.where(is_first & (line_owner == me), 1.0, 0.0)
    earlier = lax.broadcasted_iota(jnp.int32, (number, number), 0) < lax.broadcasted_iota(
        jnp.int32, (number, number), 1
    )
    earlier = jnp.where(earlier, 1.0, 0.0).astype(BF)
    rank = jnp.dot(
        jnp.broadcast_to(held, (8, number)).astype(BF), earlier, preferred_element_type=F32
    )[0:1]
    slot_no = lax.broadcasted_iota(jnp.int32, (SLOTS, number), 0).astype(F32)
    local = jnp.sum(
        jnp.where((held > 0.0) & (rank == slot_no), line_id - me * float(SHARD), 0.0),
        axis=1,
        keepdims=True,
    )
    entry = lax.broadcasted_iota(jnp.int32, (SLOTS, SHARD_WHOLE), 1).astype(F32)
    take = jnp.where(entry == local, 1.0, 0.0).astype(BF)
    tail = lax.broadcasted_iota(jnp.int32, (SLOTS, 16), 1).astype(F32) + float(SHARD_WHOLE)
    take_tail = jnp.where(tail == local, 1.0, 0.0).astype(BF)
    shard_copy.wait()
    tail_v[...] = jnp.zeros_like(tail_v)
    tail_v[0 : SHARD - SHARD_WHOLE, :] = shard_v[SHARD_WHOLE:SHARD, :]
    rows = jnp.dot(take, shard_v[0:SHARD_WHOLE, :], preferred_element_type=F32)
    rows = rows + jnp.dot(take_tail, tail_v[...], preferred_element_type=F32)
    rows = rows.astype(BF)
    for k in range(GRP):
        rows_v[k] = rows[:, k * D : (k + 1) * D]

    def send_rows(j, c):
        g2 = ((z + j // SLICES) % PLANES) * SLICES + slice_at(j % SLICES)
        remote(rows_v.at[g2], ebuf.at[g], e_send, e_recv, a, g2).start()
        return c

    lax.fori_loop(1, GRP, send_rows, 0)
    send_weights(0, 1)

    ebuf[g] = rows_v[g]

    most = jnp.zeros((ALL, 1), F32)
    for k in range(DP):
        owner = owner_of(columns[k])
        before = is_first & (line_owner == owner) & (line_of < first_column[k])
        slot = jnp.sum(jnp.where(before, 1.0, 0.0), axis=1, keepdims=True)
        most = jnp.maximum(most, slot)
        source = owner - (a * GRP).astype(F32)
        ours = (source >= 0.0) & (source < float(GRP)) & (slot < float(SLOTS))
        want = jnp.where(ours, source * float(SLOTS) + slot, -1.0)
        place = lax.broadcasted_iota(jnp.int32, (ALL, GRP * SLOTS), 1).astype(F32)
        chosen_v[k] = jnp.where(place == want, 1.0, 0.0).astype(BF)
    most_ref[0] = jnp.max(most).astype(jnp.int32)

    wait_bytes(ebuf.at[pl.ds(0, GRP - 1)], e_recv)
    table = ebuf[...].reshape(GRP * SLOTS, D)

    def picked(a2):
        return jnp.dot(chosen_v[a2], table, preferred_element_type=F32)

    for j in range(1, DP):
        a2 = (a + j) % DP
        tbuf[j] = picked(a2).astype(BF)
        remote(tbuf.at[j], dbuf.at[j], d_send, d_recv, a2, g).start()
    mine = picked(a) + extra_ref[...]
    wait_bytes(dbuf.at[pl.ds(1, DP - 1)], d_recv)
    for j in range(1, DP):
        mine = mine + dbuf[j].astype(F32)
    stream[...] = mine

    row32 = lax.broadcasted_iota(jnp.int32, (TOKENS, ALL), 0)
    lane32 = lax.broadcasted_iota(jnp.int32, (TOKENS, ALL), 1)
    own_token = lane32 == row32 + z * TOKENS

    def split(value):
        high = value.astype(BF).astype(F32)
        return jnp.concatenate([high, value - high], axis=0).astype(BF)

    for l in range(DECODER_LAYERS):
        s = stream[...]
        square = s * s
        high = square.astype(BF)
        low = (square - high.astype(F32)).astype(BF)
        ones = jnp.ones((8, D), BF)
        contract = (((1,), (1,)), ((), ()))
        sums = lax.dot_general(ones, high, contract, preferred_element_type=F32)
        sums = sums + lax.dot_general(ones, low, contract, preferred_element_type=F32)
        p1s[l, 0:ALL, :] = (s * gain_ref[l]).astype(BF)
        p1s[l, ALL : ALL + 16, :] = split(sums)

        def send_stream(j, c):
            remote(
                p1s.at[l], p1r.at[l, t], p1_send.at[l], p1_recv.at[l], a, z * SLICES + slice_at(j)
            ).start()
            return c

        for j in FAR_FIRST:
            send_stream(j, 0)
        p1r[l, t] = p1s[l]
        forward_weights(l, 0)
        wait_bytes(p1r.at[l, pl.ds(0, SLICES - 1)], p1_recv.at[l])
        await_weights(l, 0)
        if l + 1 < DECODER_LAYERS:
            send_weights(l + 1, 0)
        if l + 1 < DECODER_LAYERS:
            send_weights(l + 1, 1)

        left = jnp.concatenate([p1r[l, j, 0:ALL, :] for j in range(SLICES)], axis=1)
        sums = jnp.zeros((8, ALL), F32)
        for j in range(SLICES):
            tile = p1r[l, j, ALL : ALL + 16, :].astype(F32)
            sums = sums + tile[0:8] + tile[8:16]
        projected = jnp.dot(
            left, wqx[l].reshape(SLICES * D, QKV), preferred_element_type=F32
        ).astype(BF)
        sums = split(sums)
        for r in range(PLANES):
            for c in range(QKV // D):
                p2s[l, r, c * TOKENS : (c + 1) * TOKENS, :] = projected[
                    r * TOKENS : (r + 1) * TOKENS, c * D : (c + 1) * D
                ]
            p2s[l, r, 192:208, :] = sums
        for j in (2, 1, 3):
            z2 = (z + j) % PLANES
            remote(
                p2s.at[l, z2], p2r.at[l, j], p2_send.at[l], p2_recv.at[l], a, z2 * SLICES + t
            ).start()
        forward_weights(l, 1)
        wait_bytes(p2r.at[l, pl.ds(1, PLANES - 1)], p2_recv.at[l])
        total = p2s[l, z].astype(F32)
        for j in range(1, PLANES):
            total = total + p2r[l, j].astype(F32)

        line = total[192:193] + total[200:201]
        column = jnp.sum(
            jnp.where(own_token, jnp.broadcast_to(line, (TOKENS, ALL)), 0.0), axis=1, keepdims=True
        )
        factor = lax.rsqrt(column * (1.0 / MODEL_WIDTH) + EPSILON)
        cosine, sine = cos_ref[...], sin_ref[...]

        def rotated(block):
            return block * cosine + pltpu.roll(block, 64, 1) * sine

        for h in range(4):
            qs[h * TOKENS : (h + 1) * TOKENS, :] = rotated(
                total[h * TOKENS : (h + 1) * TOKENS] * factor
            )
        kvs[0, 96:128, :] = rotated(total[128:160] * factor)
        kvs[1, 96:128, :] = total[160:192] * factor
        pltpu.make_async_copy(cache_ref.at[l], cache_v.at[l], cache_sem.at[l]).wait()
        fresh_row = lax.broadcasted_iota(jnp.int32, (16, D), 0) >= 12
        place = lax.broadcasted_iota(jnp.int32, (16, CACHE), 1)
        step = lax.broadcasted_iota(jnp.int32, (16, CACHE), 0) % DECODE_STEPS
        fresh_live = (place >= FRESH_AT) & (place - FRESH_AT <= step)
        for b in range(REPLICA_ROWS):
            for k in range(2):
                old = cache_v[l, b, CACHE - 16 : CACHE, k * D : (k + 1) * D].astype(F32)
                new = kvs[k, pl.ds(b, 16, stride=8), :]
                cache_v[l, b, CACHE - 16 : CACHE, k * D : (k + 1) * D] = jnp.where(
                    fresh_row, new, old
                ).astype(BF)
        for b in range(REPLICA_ROWS):
            query = qs[pl.ds(b, 16, stride=8), :].astype(BF)
            scores = lax.dot_general(
                query, cache_v[l, b, :, 0:D], contract, preferred_element_type=F32
            ) * (HEAD_SIZE**-0.5)
            live = (place < len_ref[b]) | fresh_live
            scores = jnp.where(live, scores, -1e30)
            top = jnp.max(scores, axis=1, keepdims=True)
            power = jnp.exp(scores - top)
            whole = jnp.sum(power, axis=1, keepdims=True)
            value = jnp.dot(power.astype(BF), cache_v[l, b, :, D : 2 * D], preferred_element_type=F32)
            atts[pl.ds(b, 16, stride=8), :] = value / whole

        p3s[l] = atts[...].astype(BF)
        for j in (2, 1, 3):
            z2 = (z + j) % PLANES
            remote(
                p3s.at[l], p3r.at[l, z], p3_send.at[l], p3_recv.at[l], a, z2 * SLICES + t
            ).start()
        p3r[l, z] = p3s[l]
        await_weights(l, 1)
        wait_bytes(p3r.at[l, pl.ds(0, PLANES - 1)], p3_recv.at[l])
        left = jnp.concatenate(
            [
                jnp.concatenate(
                    [p3r[l, r, h * TOKENS : (h + 1) * TOKENS, :] for r in range(PLANES)], axis=0
                )
                for h in range(4)
            ],
            axis=1,
        )

        def partial(t2):
            return lax.dot_general(left, wox[l, t2], contract, preferred_element_type=F32)

        for j in FAR_FIRST:
            t2 = slice_at(j)
            p4s[l, j] = partial(t2).astype(BF)
            remote(
                p4s.at[l, j], p4r.at[l, j], p4_send.at[l], p4_recv.at[l], a, z * SLICES + t2
            ).start()
        s = stream[...] + partial(t)
        wait_bytes(p4r.at[l, pl.ds(1, SLICES - 1)], p4_recv.at[l])
        for j in range(1, SLICES):
            s = s + p4r[l, j].astype(F32)
        stream[...] = s

    last[...] = stream[...].astype(BF)
    home = g // 4
    for j in range(PLANES):
        r = (z + j) % PLANES
        g2 = r * SLICES + home
        tokens = last.at[pl.ds(pl.multiple_of(r * TOKENS, TOKENS), TOKENS), :]

        @pl.when(g2 != g)
        def _():
            remote(tokens, final.at[g % 4], o_send, o_recv, a, g2).start()

        @pl.when(g2 == g)
        def _():
            pltpu.make_async_copy(tokens, final.at[g % 4], o_recv).start()

    wait_bytes(final, o_recv)
    for k in range(4):
        out_ref[:, k * D : (k + 1) * D] = final[k]

    wait_bytes(land.at[pl.ds(0, DP - 1)], i_send)
    wait_bytes(ebuf.at[pl.ds(0, GRP - 1)], e_send)
    wait_bytes(dbuf.at[pl.ds(1, DP - 1)], d_send)
    for l in range(DECODER_LAYERS):
        for kind in range(2):
            buf = (wqx, wox)[kind]
            wait_bytes(buf.at[l, pl.ds(0, SLICES - 1), half, :], w_send.at[l, kind])
            wait_bytes(buf.at[l, :, half, :], f_send.at[l, kind])
        wait_bytes(p1r.at[l, pl.ds(0, SLICES - 1)], p1_send.at[l])
        wait_bytes(p2r.at[l, pl.ds(1, PLANES - 1)], p2_send.at[l])
        wait_bytes(p3r.at[l, pl.ds(0, PLANES - 1)], p3_send.at[l])
        wait_bytes(p4r.at[l, pl.ds(1, SLICES - 1)], p4_send.at[l])

    @pl.when(home == t)
    def _():
        wait_bytes(final.at[pl.ds(0, PLANES - 1)], o_send)

    @pl.when(home != t)
    def _():
        wait_bytes(final, o_send)


def decode(ids, extra, gain, cosine, sine, lengths, wq, wo, cache, embed):
    vmem = pl.BlockSpec(memory_space=pltpu.VMEM)
    hbm = pl.BlockSpec(memory_space=pltpu.HBM)
    layers = DECODER_LAYERS
    dma = pltpu.SemaphoreType.DMA
    return pl.pallas_call(
        main_kernel,
        out_shape=(
            jax.ShapeDtypeStruct((TOKENS, 512), BF),
            jax.ShapeDtypeStruct((DP, 8, ALL), jnp.int32),
            jax.ShapeDtypeStruct((1,), jnp.int32),
        ),
        in_specs=[
            vmem,
            vmem,
            vmem,
            vmem,
            vmem,
            pl.BlockSpec(memory_space=pltpu.SMEM),
            hbm,
            hbm,
            hbm,
            hbm,
        ],
        out_specs=(vmem, vmem, pl.BlockSpec(memory_space=pltpu.SMEM)),
        scratch_shapes=[
            pltpu.VMEM((layers, REPLICA_ROWS, CACHE, 2 * D), BF),
            pltpu.VMEM((SHARD, MODEL_WIDTH), BF),
            pltpu.VMEM((DP, 8, ALL), jnp.int32),
            pltpu.VMEM((16, MODEL_WIDTH), BF),
            pltpu.VMEM((GRP, SLOTS, D), BF),
            pltpu.VMEM((DP, ALL, GRP * SLOTS), BF),
            pltpu.VMEM((layers, SLICES, D, QKV), BF),
            pltpu.VMEM((layers, SLICES, D, 512), BF),
            pltpu.VMEM((GRP, SLOTS, D), BF),
            pltpu.VMEM((DP, ALL, D), BF),
            pltpu.VMEM((DP, ALL, D), BF),
            pltpu.VMEM((ALL, D), F32),
            pltpu.VMEM((layers, ALL + 16, D), BF),
            pltpu.VMEM((layers, SLICES, ALL + 16, D), BF),
            pltpu.VMEM((layers, PLANES, 208, D), BF),
            pltpu.VMEM((layers, PLANES, 208, D), BF),
            pltpu.VMEM((4 * TOKENS, D), F32),
            pltpu.VMEM((2, 16 * REPLICA_ROWS, D), F32),
            pltpu.VMEM((4 * TOKENS, D), F32),
            pltpu.VMEM((layers, 4 * TOKENS, D), BF),
            pltpu.VMEM((layers, PLANES, 4 * TOKENS, D), BF),
            pltpu.VMEM((layers, SLICES, ALL, D), BF),
            pltpu.VMEM((layers, SLICES, ALL, D), BF),
            pltpu.VMEM((ALL, D), BF),
            pltpu.VMEM((4, TOKENS, D), BF),
            dma((layers,)),
            dma((layers, 2)),
            dma((layers, 2)),
            dma((layers, 2)),
            dma((layers, 2)),
            dma,
            dma,
            dma,
            dma,
            dma((layers,)),
            dma((layers,)),
            dma((layers,)),
            dma((layers,)),
            dma((layers,)),
            dma((layers,)),
            dma((layers,)),
            dma((layers,)),
            dma,
            dma,
            dma,
            dma,
            dma,
        ],
        compiler_params=pltpu.CompilerParams(
            collective_id=1, has_side_effects=True, vmem_limit_bytes=48 * 1024 * 1024
        ),
        name="decode",
    )(ids, extra, gain, cosine, sine, lengths, wq, wo, cache, embed)


def body(
    token_ids,
    start_pos,
    cache_len,
    embed_table,
    norm_gain,
    query_key_value_weight,
    output_weight,
    key_value_cache,
):
    a, g = lax.axis_index("dp"), lax.axis_index("grp")
    z = g // SLICES
    me = a * GRP + g
    shard_rows = embed_table.shape[0]
    number = DP * ALL

    lengths = lax.dynamic_index_in_dim(cache_len[0], z, 0, keepdims=False)
    starts = lax.dynamic_index_in_dim(start_pos[0], z, 0, keepdims=False)
    position = (starts[None, :] + jnp.arange(DECODE_STEPS, dtype=jnp.int32)[:, None]).reshape(TOKENS)
    exponent = jnp.arange(HEAD_SIZE // 2, dtype=F32) * (2.0 / HEAD_SIZE)
    frequency = jnp.power(F32(ROPE_BASE), -exponent)
    angles = position.astype(F32)[:, None] * frequency
    cosine, sine = jnp.cos(angles), jnp.sin(angles)
    cosine = jnp.concatenate([cosine, cosine], axis=1)
    sine = jnp.concatenate([-sine, sine], axis=1)
    gain = lax.dynamic_slice_in_dim(norm_gain, g * D, D, 1).reshape(DECODER_LAYERS, 1, D)

    def run(extra):
        return decode(
            ids,
            extra,
            gain,
            cosine,
            sine,
            lengths,
            query_key_value_weight,
            output_weight,
            key_value_cache.reshape(DECODER_LAYERS, REPLICA_ROWS, CACHE, 2 * D),
            embed_table,
        )

    ids = jnp.broadcast_to(token_ids[0].transpose(0, 2, 1).reshape(1, ALL), (8, ALL))
    out, everyone, most = run(jnp.zeros((ALL, D), F32))

    def again(_):
        flat = everyone[:, 0, :].reshape(DP * ALL)
        owner = flat // shard_rows
        order = jnp.arange(DP * ALL, dtype=jnp.int32)
        first = jnp.min(jnp.where(flat[:, None] == flat[None, :], order[None, :], DP * ALL), axis=1)
        before = (
            (first == order)[None, :]
            & (owner[:, None] == owner[None, :])
            & (order[None, :] < first[:, None])
        )
        slot = jnp.sum(before.astype(jnp.int32), axis=1)
        late = (owner == me) & (slot >= SLOTS)
        more = jnp.take(embed_table, jnp.where(late, flat - me * shard_rows, 0), axis=0, mode="clip")
        more = jnp.where(late[:, None], more, jnp.zeros_like(more)).reshape(DP, ALL, GRP, D)
        more = more.transpose(0, 2, 1, 3).reshape(DP * GRP, ALL, D)
        more = lax.all_to_all(more, ("dp", "grp"), split_axis=0, concat_axis=0, tiled=True)
        return run(jnp.sum(more.astype(F32), axis=0))[0]

    out = lax.cond(most[0] >= SLOTS, again, lambda _: out, jnp.int32(0))
    return out.reshape(DECODE_STEPS, REPLICA_ROWS, 512).transpose(1, 0, 2)[:, None]


def solution(mesh):
    return jax.shard_map(
        body,
        mesh=mesh,
        in_specs=(
            P("dp", None, None, None),
            P("dp", None, None),
            P("dp", None, None),
            P(("dp", "grp"), None),
            P(),
            P(None, "grp", None),
            P(None, "grp", None),
            P(None, "dp", "grp", None, None),
        ),
        out_specs=P("dp", "grp", None, None),
        check_vma=False,
    )
```

```python
import jax
import jax.numpy as jnp
from jax import lax
from jax.experimental import pallas as pl
from jax.experimental.pallas import tpu as pltpu
from jax.sharding import PartitionSpec as P

MODEL_WIDTH = 4096
QUERY_HEADS = 32
KEY_VALUE_HEADS = 8
HEAD_SIZE = 128
DECODER_LAYERS = 2
DECODE_STEPS = 4
REPLICA_ROWS = 8
ROPE_BASE = 500000.0
EPSILON = 1e-05

MESH = pl.DeviceIdType.MESH
SLOTS = 16
DP = 4
PLANES = 4
SLICES = 8
GRP = PLANES * SLICES
FAR_FIRST = (6, 5, 7, 2, 4, 1, 3)
TOKENS = REPLICA_ROWS * DECODE_STEPS
ALL = PLANES * TOKENS
D = 128
QKV = 768
CACHE = 1024
SHARD = 1002
SHARD_WHOLE = 992
FRESH_AT = CACHE - DECODE_STEPS
BF = jnp.bfloat16
F32 = jnp.float32


def main_kernel(
    ids_ref,
    extra_ref,
    gain_ref,
    cos_ref,
    sin_ref,
    len_ref,
    wq_ref,
    wo_ref,
    cache_ref,
    embed_ref,
    out_ref,
    all_ref,
    most_ref,
    cache_v,
    shard_v,
    land,
    tail_v,
    rows_v,
    chosen_v,
    wqx,
    wox,
    ebuf,
    tbuf,
    dbuf,
    stream,
    p1s,
    p1r,
    p2s,
    p2r,
    qs,
    kvs,
    atts,
    p3s,
    p3r,
    p4s,
    p4r,
    last,
    final,
    cache_sem,
    w_send,
    w_recv,
    f_send,
    f_recv,
    e_send,
    e_recv,
    d_send,
    d_recv,
    p1_send,
    p1_recv,
    p2_send,
    p2_recv,
    p3_send,
    p3_recv,
    p4_send,
    p4_recv,
    o_send,
    o_recv,
    i_send,
    i_recv,
    s_sem,
):
    a, g = lax.axis_index("dp"), lax.axis_index("grp")
    core = a % 2
    sibling = a + 1 - 2 * core
    z, t = g // SLICES, g % SLICES
    y, x = t // 4, t % 4

    def remote(src, dst, send_sem, recv_sem, a2, g2):
        return pltpu.make_async_remote_copy(
            src_ref=src,
            dst_ref=dst,
            send_sem=send_sem,
            recv_sem=recv_sem,
            device_id=(a2, g2),
            device_id_type=MESH,
        )

    def wait_bytes(ref, sem):
        pltpu.make_async_copy(ref, ref, sem).wait()

    def slice_at(j):
        return ((y + j // 4) % 2) * 4 + (x + j % 4) % 4

    shard_copy = pltpu.make_async_copy(embed_ref, shard_v, s_sem)
    shard_copy.start()
    for l in range(DECODER_LAYERS):
        pltpu.make_async_copy(cache_ref.at[l], cache_v.at[l], cache_sem.at[l]).start()

    barrier = pltpu.get_barrier_semaphore()

    def greet(j, c):
        pl.semaphore_signal(barrier, inc=1, device_id=(a, (g + j) % GRP), device_id_type=MESH)
        return c

    lax.fori_loop(1, GRP, greet, 0)
    for j in range(1, DP):
        pl.semaphore_signal(barrier, inc=1, device_id=((a + j) % DP, g), device_id_type=MESH)

    def greet_across(k, c):
        g2 = z * SLICES + (1 - y) * 4 + k
        pl.semaphore_signal(barrier, inc=1, device_id=((a + 2) % DP, g2), device_id_type=MESH)
        return c

    lax.fori_loop(0, 4, greet_across, 0)
    pl.semaphore_wait(barrier, GRP - 1 + DP - 1 + 4)

    land[a] = ids_ref[...]
    for j in range(1, DP):
        remote(ids_ref, land.at[a], i_send, i_recv, (a + j) % DP, g).start()

    half = pl.ds(pl.multiple_of(core * 64, 64), 64)
    halves = [pl.ds(pl.multiple_of(core * 64 + k * 32, 32), 32) for k in range(2)]
    across = (a + 2) % DP

    def qkv_pieces(l, t2, half):
        return (
            (
                wq_ref.at[l, half, pl.ds(pl.multiple_of(t2 * 512, 512), 512)],
                wqx.at[l, t, half, pl.ds(0, 512)],
            ),
            (
                wq_ref.at[l, half, pl.ds(pl.multiple_of(4096 + t2 * 128, 128), 128)],
                wqx.at[l, t, half, pl.ds(512, 128)],
            ),
            (
                wq_ref.at[l, half, pl.ds(pl.multiple_of(5120 + t2 * 128, 128), 128)],
                wqx.at[l, t, half, pl.ds(640, 128)],
            ),
        )

    def out_pieces(l, t2, half):
        return (
            (
                wo_ref.at[l, half, pl.ds(pl.multiple_of(t2 * 512, 512), 512)],
                wox.at[l, t, half, :],
            ),
        )

    def send_weights(l, kind):
        pieces = (qkv_pieces, out_pieces)[kind]

        def send(j, rows, a2):
            t2 = slice_at(j)
            for src, dst in pieces(l, t2, rows):
                remote(src, dst, w_send.at[l, kind], w_recv.at[l, kind], a2, z * SLICES + t2).start()

        def one(j, c):
            send(j, half, a)
            return c

        def both(j, c):
            send(j, halves[0], a)
            send(j, halves[1], across)
            return c

        for j in FAR_FIRST:
            (both if j >= 4 else one)(j, 0)
        for src, dst in pieces(l, t, half):
            pltpu.make_async_copy(src, dst, w_recv.at[l, kind]).start()

    def forward_weights(l, kind):
        buf = (wqx, wox)[kind]
        wait_bytes(buf.at[l, :, half, :], w_recv.at[l, kind])
        remote(
            buf.at[l, :, half, :],
            buf.at[l, :, half, :],
            f_send.at[l, kind],
            f_recv.at[l, kind],
            sibling,
            g,
        ).start()

    def await_weights(l, kind):
        buf = (wqx, wox)[kind]
        wait_bytes(buf.at[l, :, half, :], f_recv.at[l, kind])

    send_weights(0, 0)
    kvs[...] = jnp.zeros_like(kvs)
    wait_bytes(land.at[pl.ds(0, DP - 1)], i_recv)

    number = DP * ALL
    all_ref[...] = land[...]
    along = jnp.concatenate([land[k] for k in range(DP)], axis=1).astype(F32)
    line_of = lax.broadcasted_iota(jnp.int32, (1, number), 1).astype(F32)
    line_id = along[0:1]
    columns = []
    for k in range(DP):
        square = jnp.concatenate([along[:, k * ALL : (k + 1) * ALL]] * 16, axis=0)
        columns.append(jnp.transpose(square)[:, 0:1])

    def owner_of(ids):
        return jnp.floor((ids + 0.5) * (1.0 / SHARD))

    first_line = jnp.full((1, number), float(number), F32)
    first_column = []
    for k in range(DP):
        same = columns[k] == line_id
        up = lax.broadcasted_iota(jnp.int32, (ALL, number), 0).astype(F32) + float(k * ALL)
        first_line = jnp.minimum(
            first_line, jnp.min(jnp.where(same, up, float(number)), axis=0, keepdims=True)
        )
        first_column.append(jnp.min(jnp.where(same, line_of, float(number)), axis=1, keepdims=True))
    is_first = first_line == line_of
    line_owner = owner_of(line_id)
    me = (a * GRP + g).astype(F32)

    held = jnp.where(is_first & (line_owner == me), 1.0, 0.0)
    earlier = lax.broadcasted_iota(jnp.int32, (number, number), 0) < lax.broadcasted_iota(
        jnp.int32, (number, number), 1
    )
    earlier = jnp.where(earlier, 1.0, 0.0).astype(BF)
    rank = jnp.dot(
        jnp.broadcast_to(held, (8, number)).astype(BF), earlier, preferred_element_type=F32
    )[0:1]
    slot_no = lax.broadcasted_iota(jnp.int32, (SLOTS, number), 0).astype(F32)
    local = jnp.sum(
        jnp.where((held > 0.0) & (rank == slot_no), line_id - me * float(SHARD), 0.0),
        axis=1,
        keepdims=True,
    )
    entry = lax.broadcasted_iota(jnp.int32, (SLOTS, SHARD_WHOLE), 1).astype(F32)
    take = jnp.where(entry == local, 1.0, 0.0).astype(BF)
    tail = lax.broadcasted_iota(jnp.int32, (SLOTS, 16), 1).astype(F32) + float(SHARD_WHOLE)
    take_tail = jnp.where(tail == local, 1.0, 0.0).astype(BF)
    shard_copy.wait()
    tail_v[...] = jnp.zeros_like(tail_v)
    tail_v[0 : SHARD - SHARD_WHOLE, :] = shard_v[SHARD_WHOLE:SHARD, :]
    rows = jnp.dot(take, shard_v[0:SHARD_WHOLE, :], preferred_element_type=F32)
    rows = rows + jnp.dot(take_tail, tail_v[...], preferred_element_type=F32)
    rows = rows.astype(BF)
    for k in range(GRP):
        rows_v[k] = rows[:, k * D : (k + 1) * D]

    def send_rows(j, c):
        g2 = ((z + j // SLICES) % PLANES) * SLICES + slice_at(j % SLICES)
        remote(rows_v.at[g2], ebuf.at[g], e_send, e_recv, a, g2).start()
        return c

    for j in FAR_FIRST + (0,):
        for k in (2, 1, 3, 0):
            if j + k > 0:
                send_rows(k * SLICES + j, 0)
    send_weights(0, 1)

    ebuf[g] = rows_v[g]

    most = jnp.zeros((ALL, 1), F32)
    for k in range(DP):
        owner = owner_of(columns[k])
        before = is_first & (line_owner == owner) & (line_of < first_column[k])
        slot = jnp.sum(jnp.where(before, 1.0, 0.0), axis=1, keepdims=True)
        most = jnp.maximum(most, slot)
        source = owner - (a * GRP).astype(F32)
        ours = (source >= 0.0) & (source < float(GRP)) & (slot < float(SLOTS))
        want = jnp.where(ours, source * float(SLOTS) + slot, -1.0)
        place = lax.broadcasted_iota(jnp.int32, (ALL, GRP * SLOTS), 1).astype(F32)
        chosen_v[k] = jnp.where(place == want, 1.0, 0.0).astype(BF)
    most_ref[0] = jnp.max(most).astype(jnp.int32)

    wait_bytes(ebuf.at[pl.ds(0, GRP - 1)], e_recv)
    table = ebuf[...].reshape(GRP * SLOTS, D)

    def picked(a2):
        return jnp.dot(chosen_v[a2], table, preferred_element_type=F32)

    for j in range(1, DP):
        a2 = (a + j) % DP
        tbuf[j] = picked(a2).astype(BF)
        remote(tbuf.at[j], dbuf.at[j], d_send, d_recv, a2, g).start()
    mine = picked(a) + extra_ref[...]
    wait_bytes(dbuf.at[pl.ds(1, DP - 1)], d_recv)
    for j in range(1, DP):
        mine = mine + dbuf[j].astype(F32)
    stream[...] = mine

    row32 = lax.broadcasted_iota(jnp.int32, (TOKENS, ALL), 0)
    lane32 = lax.broadcasted_iota(jnp.int32, (TOKENS, ALL), 1)
    own_token = lane32 == row32 + z * TOKENS

    def split(value):
        high = value.astype(BF).astype(F32)
        return jnp.concatenate([high, value - high], axis=0).astype(BF)

    for l in range(DECODER_LAYERS):
        s = stream[...]
        square = s * s
        high = square.astype(BF)
        low = (square - high.astype(F32)).astype(BF)
        ones = jnp.ones((8, D), BF)
        contract = (((1,), (1,)), ((), ()))
        sums = lax.dot_general(ones, high, contract, preferred_element_type=F32)
        sums = sums + lax.dot_general(ones, low, contract, preferred_element_type=F32)
        p1s[l, 0:ALL, :] = (s * gain_ref[l]).astype(BF)
        p1s[l, ALL : ALL + 16, :] = split(sums)

        def send_stream(j, c):
            remote(
                p1s.at[l], p1r.at[l, t], p1_send.at[l], p1_recv.at[l], a, z * SLICES + slice_at(j)
            ).start()
            return c

        for j in FAR_FIRST:
            send_stream(j, 0)
        p1r[l, t] = p1s[l]
        forward_weights(l, 0)
        wait_bytes(p1r.at[l, pl.ds(0, SLICES - 1)], p1_recv.at[l])
        await_weights(l, 0)
        if l + 1 < DECODER_LAYERS:
            send_weights(l + 1, 0)
        if l + 1 < DECODER_LAYERS:
            send_weights(l + 1, 1)

        left = jnp.concatenate([p1r[l, j, 0:ALL, :] for j in range(SLICES)], axis=1)
        sums = jnp.zeros((8, ALL), F32)
        for j in range(SLICES):
            tile = p1r[l, j, ALL : ALL + 16, :].astype(F32)
            sums = sums + tile[0:8] + tile[8:16]
        projected = jnp.dot(
            left, wqx[l].reshape(SLICES * D, QKV), preferred_element_type=F32
        ).astype(BF)
        sums = split(sums)
        for r in range(PLANES):
            for c in range(QKV // D):
                p2s[l, r, c * TOKENS : (c + 1) * TOKENS, :] = projected[
                    r * TOKENS : (r + 1) * TOKENS, c * D : (c + 1) * D
                ]
            p2s[l, r, 192:208, :] = sums
        for j in (2, 1, 3):
            z2 = (z + j) % PLANES
            remote(
                p2s.at[l, z2], p2r.at[l, j], p2_send.at[l], p2_recv.at[l], a, z2 * SLICES + t
            ).start()
        forward_weights(l, 1)
        wait_bytes(p2r.at[l, pl.ds(1, PLANES - 1)], p2_recv.at[l])
        total = p2s[l, z].astype(F32)
        for j in range(1, PLANES):
            total = total + p2r[l, j].astype(F32)

        line = total[192:193] + total[200:201]
        column = jnp.sum(
            jnp.where(own_token, jnp.broadcast_to(line, (TOKENS, ALL)), 0.0), axis=1, keepdims=True
        )
        factor = lax.rsqrt(column * (1.0 / MODEL_WIDTH) + EPSILON)
        cosine, sine = cos_ref[...], sin_ref[...]

        def rotated(block):
            return block * cosine + pltpu.roll(block, 64, 1) * sine

        for h in range(4):
            qs[h * TOKENS : (h + 1) * TOKENS, :] = rotated(
                total[h * TOKENS : (h + 1) * TOKENS] * factor
            )
        kvs[0, 96:128, :] = rotated(total[128:160] * factor)
        kvs[1, 96:128, :] = total[160:192] * factor
        pltpu.make_async_copy(cache_ref.at[l], cache_v.at[l], cache_sem.at[l]).wait()
        fresh_row = lax.broadcasted_iota(jnp.int32, (16, D), 0) >= 12
        place = lax.broadcasted_iota(jnp.int32, (16, CACHE), 1)
        step = lax.broadcasted_iota(jnp.int32, (16, CACHE), 0) % DECODE_STEPS
        fresh_live = (place >= FRESH_AT) & (place - FRESH_AT <= step)
        for b in range(REPLICA_ROWS):
            for k in range(2):
                old = cache_v[l, b, CACHE - 16 : CACHE, k * D : (k + 1) * D].astype(F32)
                new = kvs[k, pl.ds(b, 16, stride=8), :]
                cache_v[l, b, CACHE - 16 : CACHE, k * D : (k + 1) * D] = jnp.where(
                    fresh_row, new, old
                ).astype(BF)
        for b in range(REPLICA_ROWS):
            query = qs[pl.ds(b, 16, stride=8), :].astype(BF)
            scores = lax.dot_general(
                query, cache_v[l, b, :, 0:D], contract, preferred_element_type=F32
            ) * (HEAD_SIZE**-0.5)
            live = (place < len_ref[b]) | fresh_live
            scores = jnp.where(live, scores, -1e30)
            top = jnp.max(scores, axis=1, keepdims=True)
            power = jnp.exp(scores - top)
            whole = jnp.sum(power, axis=1, keepdims=True)
            value = jnp.dot(power.astype(BF), cache_v[l, b, :, D : 2 * D], preferred_element_type=F32)
            atts[pl.ds(b, 16, stride=8), :] = value / whole

        p3s[l] = atts[...].astype(BF)
        for j in (2, 1, 3):
            z2 = (z + j) % PLANES
            remote(
                p3s.at[l], p3r.at[l, z], p3_send.at[l], p3_recv.at[l], a, z2 * SLICES + t
            ).start()
        p3r[l, z] = p3s[l]
        await_weights(l, 1)
        wait_bytes(p3r.at[l, pl.ds(0, PLANES - 1)], p3_recv.at[l])
        left = jnp.concatenate(
            [
                jnp.concatenate(
                    [p3r[l, r, h * TOKENS : (h + 1) * TOKENS, :] for r in range(PLANES)], axis=0
                )
                for h in range(4)
            ],
            axis=1,
        )

        def partial(t2):
            return lax.dot_general(left, wox[l, t2], contract, preferred_element_type=F32)

        for j in FAR_FIRST:
            t2 = slice_at(j)
            p4s[l, j] = partial(t2).astype(BF)
            remote(
                p4s.at[l, j], p4r.at[l, j], p4_send.at[l], p4_recv.at[l], a, z * SLICES + t2
            ).start()
        s = stream[...] + partial(t)
        wait_bytes(p4r.at[l, pl.ds(1, SLICES - 1)], p4_recv.at[l])
        for j in range(1, SLICES):
            s = s + p4r[l, j].astype(F32)
        stream[...] = s

    last[...] = stream[...].astype(BF)
    home = g // 4
    for j in range(PLANES):
        r = (z + j) % PLANES
        g2 = r * SLICES + home
        tokens = last.at[pl.ds(pl.multiple_of(r * TOKENS, TOKENS), TOKENS), :]

        @pl.when(g2 != g)
        def _():
            remote(tokens, final.at[g % 4], o_send, o_recv, a, g2).start()

        @pl.when(g2 == g)
        def _():
            pltpu.make_async_copy(tokens, final.at[g % 4], o_recv).start()

    wait_bytes(final, o_recv)
    for k in range(4):
        out_ref[:, k * D : (k + 1) * D] = final[k]

    wait_bytes(land.at[pl.ds(0, DP - 1)], i_send)
    wait_bytes(ebuf.at[pl.ds(0, GRP - 1)], e_send)
    wait_bytes(dbuf.at[pl.ds(1, DP - 1)], d_send)
    for l in range(DECODER_LAYERS):
        for kind in range(2):
            buf = (wqx, wox)[kind]
            wait_bytes(buf.at[l, pl.ds(0, SLICES - 1), half, :], w_send.at[l, kind])
            wait_bytes(buf.at[l, :, half, :], f_send.at[l, kind])
        wait_bytes(p1r.at[l, pl.ds(0, SLICES - 1)], p1_send.at[l])
        wait_bytes(p2r.at[l, pl.ds(1, PLANES - 1)], p2_send.at[l])
        wait_bytes(p3r.at[l, pl.ds(0, PLANES - 1)], p3_send.at[l])
        wait_bytes(p4r.at[l, pl.ds(1, SLICES - 1)], p4_send.at[l])

    @pl.when(home == t)
    def _():
        wait_bytes(final.at[pl.ds(0, PLANES - 1)], o_send)

    @pl.when(home != t)
    def _():
        wait_bytes(final, o_send)


def decode(ids, extra, gain, cosine, sine, lengths, wq, wo, cache, embed):
    vmem = pl.BlockSpec(memory_space=pltpu.VMEM)
    hbm = pl.BlockSpec(memory_space=pltpu.HBM)
    layers = DECODER_LAYERS
    dma = pltpu.SemaphoreType.DMA
    return pl.pallas_call(
        main_kernel,
        out_shape=(
            jax.ShapeDtypeStruct((TOKENS, 512), BF),
            jax.ShapeDtypeStruct((DP, 8, ALL), jnp.int32),
            jax.ShapeDtypeStruct((1,), jnp.int32),
        ),
        in_specs=[
            vmem,
            vmem,
            vmem,
            vmem,
            vmem,
            pl.BlockSpec(memory_space=pltpu.SMEM),
            hbm,
            hbm,
            hbm,
            hbm,
        ],
        out_specs=(vmem, vmem, pl.BlockSpec(memory_space=pltpu.SMEM)),
        scratch_shapes=[
            pltpu.VMEM((layers, REPLICA_ROWS, CACHE, 2 * D), BF),
            pltpu.VMEM((SHARD, MODEL_WIDTH), BF),
            pltpu.VMEM((DP, 8, ALL), jnp.int32),
            pltpu.VMEM((16, MODEL_WIDTH), BF),
            pltpu.VMEM((GRP, SLOTS, D), BF),
            pltpu.VMEM((DP, ALL, GRP * SLOTS), BF),
            pltpu.VMEM((layers, SLICES, D, QKV), BF),
            pltpu.VMEM((layers, SLICES, D, 512), BF),
            pltpu.VMEM((GRP, SLOTS, D), BF),
            pltpu.VMEM((DP, ALL, D), BF),
            pltpu.VMEM((DP, ALL, D), BF),
            pltpu.VMEM((ALL, D), F32),
            pltpu.VMEM((layers, ALL + 16, D), BF),
            pltpu.VMEM((layers, SLICES, ALL + 16, D), BF),
            pltpu.VMEM((layers, PLANES, 208, D), BF),
            pltpu.VMEM((layers, PLANES, 208, D), BF),
            pltpu.VMEM((4 * TOKENS, D), F32),
            pltpu.VMEM((2, 16 * REPLICA_ROWS, D), F32),
            pltpu.VMEM((4 * TOKENS, D), F32),
            pltpu.VMEM((layers, 4 * TOKENS, D), BF),
            pltpu.VMEM((layers, PLANES, 4 * TOKENS, D), BF),
            pltpu.VMEM((layers, SLICES, ALL, D), BF),
            pltpu.VMEM((layers, SLICES, ALL, D), BF),
            pltpu.VMEM((ALL, D), BF),
            pltpu.VMEM((4, TOKENS, D), BF),
            dma((layers,)),
            dma((layers, 2)),
            dma((layers, 2)),
            dma((layers, 2)),
            dma((layers, 2)),
            dma,
            dma,
            dma,
            dma,
            dma((layers,)),
            dma((layers,)),
            dma((layers,)),
            dma((layers,)),
            dma((layers,)),
            dma((layers,)),
            dma((layers,)),
            dma((layers,)),
            dma,
            dma,
            dma,
            dma,
            dma,
        ],
        compiler_params=pltpu.CompilerParams(
            collective_id=1, has_side_effects=True, vmem_limit_bytes=48 * 1024 * 1024
        ),
        name="decode",
    )(ids, extra, gain, cosine, sine, lengths, wq, wo, cache, embed)


def body(
    token_ids,
    start_pos,
    cache_len,
    embed_table,
    norm_gain,
    query_key_value_weight,
    output_weight,
    key_value_cache,
):
    a, g = lax.axis_index("dp"), lax.axis_index("grp")
    z = g // SLICES
    me = a * GRP + g
    shard_rows = embed_table.shape[0]
    number = DP * ALL

    lengths = lax.dynamic_index_in_dim(cache_len[0], z, 0, keepdims=False)
    starts = lax.dynamic_index_in_dim(start_pos[0], z, 0, keepdims=False)
    position = (starts[None, :] + jnp.arange(DECODE_STEPS, dtype=jnp.int32)[:, None]).reshape(TOKENS)
    exponent = jnp.arange(HEAD_SIZE // 2, dtype=F32) * (2.0 / HEAD_SIZE)
    frequency = jnp.power(F32(ROPE_BASE), -exponent)
    angles = position.astype(F32)[:, None] * frequency
    cosine, sine = jnp.cos(angles), jnp.sin(angles)
    cosine = jnp.concatenate([cosine, cosine], axis=1)
    sine = jnp.concatenate([-sine, sine], axis=1)
    gain = lax.dynamic_slice_in_dim(norm_gain, g * D, D, 1).reshape(DECODER_LAYERS, 1, D)

    def run(extra):
        return decode(
            ids,
            extra,
            gain,
            cosine,
            sine,
            lengths,
            query_key_value_weight,
            output_weight,
            key_value_cache.reshape(DECODER_LAYERS, REPLICA_ROWS, CACHE, 2 * D),
            embed_table,
        )

    ids = jnp.broadcast_to(token_ids[0].transpose(0, 2, 1).reshape(1, ALL), (8, ALL))
    out, everyone, most = run(jnp.zeros((ALL, D), F32))

    def again(_):
        flat = everyone[:, 0, :].reshape(DP * ALL)
        owner = flat // shard_rows
        order = jnp.arange(DP * ALL, dtype=jnp.int32)
        first = jnp.min(jnp.where(flat[:, None] == flat[None, :], order[None, :], DP * ALL), axis=1)
        before = (
            (first == order)[None, :]
            & (owner[:, None] == owner[None, :])
            & (order[None, :] < first[:, None])
        )
        slot = jnp.sum(before.astype(jnp.int32), axis=1)
        late = (owner == me) & (slot >= SLOTS)
        more = jnp.take(embed_table, jnp.where(late, flat - me * shard_rows, 0), axis=0, mode="clip")
        more = jnp.where(late[:, None], more, jnp.zeros_like(more)).reshape(DP, ALL, GRP, D)
        more = more.transpose(0, 2, 1, 3).reshape(DP * GRP, ALL, D)
        more = lax.all_to_all(more, ("dp", "grp"), split_axis=0, concat_axis=0, tiled=True)
        return run(jnp.sum(more.astype(F32), axis=0))[0]

    out = lax.cond(most[0] >= SLOTS, again, lambda _: out, jnp.int32(0))
    return out.reshape(DECODE_STEPS, REPLICA_ROWS, 512).transpose(1, 0, 2)[:, None]


def solution(mesh):
    return jax.shard_map(
        body,
        mesh=mesh,
        in_specs=(
            P("dp", None, None, None),
            P("dp", None, None),
            P("dp", None, None),
            P(("dp", "grp"), None),
            P(),
            P(None, "grp", None),
            P(None, "grp", None),
            P(None, "dp", "grp", None, None),
        ),
        out_specs=P("dp", "grp", None, None),
        check_vma=False,
    )
```
